512 devices in a mesh: island: 16 (over y, x_lo), fsdp: 32 (over x_hi, z, core).
Axes of the slice: x: 4 (x_hi: 2, x_lo: 2; x = x_hi * 2 + x_lo), y: 8, z: 8, core: 2. Of those that a mesh axis runs over, the one named last changes fastest.
Arguments:
- inner: bfloat16 [16, 1536, 3072], P('island', 'fsdp'), may hold values from -6 to 6
- outer: float32 [1536, 3072], P('fsdp'), may hold values from -6 to 6
- momentum: float32 [1536, 3072], P('fsdp'), may hold values from -4 to 4
- residual: float32 [16, 1536, 3072], P('island', 'fsdp'), may hold values from -4 to 4
Outputs:
- outer_next: float32 [1536, 3072], P('fsdp')
- momentum_next: float32 [1536, 3072], P('fsdp')
- residual_next: float32 [16, 1536, 3072], P('island', 'fsdp')
The draws below stay inside these ranges and needn't reach their ends.
All inputs are finite; a program needn't handle non-finite values.
Results may differ from the reference program's by a relative error of at most 0.0003.
Values sent between devices are 32-bit elements; how exact they have to be, the bound alone decides.
A program may use at most 64 MiB of HBM per device.

```python
import math
import jax
import jax.numpy as jnp
from jax import lax

COLS = 3072
GROUP = 128
BAND = 32
ROWS = 1536
ISLANDS = 16


def block_levels(key, extent, split, least, high):
    def one(dim, blocks):
        draws = jax.random.uniform(jax.random.fold_in(jax.random.fold_in(key, 6), dim), (blocks,), jnp.float32, least / len(split), high / len(split))
        return jnp.repeat(jnp.exp(draws), extent[dim] // blocks).reshape((-1,) + (1,) * (len(extent) - dim - 1))

    loudness = one(*split[0])
    for cut in split[1:]:
        loudness = loudness * one(*cut)
    return loudness


def gaussian(stream_key, dims, spread, limit, pieces=(), kind=jnp.bfloat16):
    entries = jax.random.normal(stream_key, dims, jnp.float32) * spread
    if len(pieces) > 0:
        entries = block_levels(stream_key, dims, pieces, -0.22, 0.18) * entries
    return jnp.clip(entries, min=-limit, max=limit).astype(kind)


def setup_inputs(seed: int = 0) -> dict:
    splits = jax.random.split(jax.random.key(seed), 5)
    return {
        "inner": gaussian(splits[0], (ISLANDS, ROWS, COLS), 1.0, 6.0, ((0, 16), (1, 32))),
        "outer": gaussian(splits[1], (ROWS, COLS), 1.0, 6.0, ((0, 32),), jnp.float32),
        "momentum": gaussian(splits[2], (ROWS, COLS), 0.5, 4.0, ((0, 32),), jnp.float32),
        "residual": gaussian(splits[3], (ISLANDS, ROWS, COLS), 0.5, 4.0, ((0, 16), (1, 32)), jnp.float32),
    }


outer_rate = 0.7
momentum_keep = 0.9

def cosine_low():
    freq = jnp.arange(GROUP, dtype=jnp.float32)[:, None]
    place = jnp.arange(GROUP, dtype=jnp.float32)[None, :]
    table = jnp.cos(math.pi * (2.0 * place + 1.0) * freq / (2.0 * GROUP))
    scale = jnp.where(freq == 0, math.sqrt(1.0 / GROUP), math.sqrt(2.0 / GROUP))
    return (table * scale)[:BAND]

def invert(low, coef):
    part = jnp.einsum('kn,...rkbl->...rnbl', low, coef, precision=lax.Precision.HIGHEST)
    whole = jnp.einsum('...rnbl,lm->...rnbm', part, low, precision=lax.Precision.HIGHEST)
    return whole.reshape(whole.shape[:-4] + (ROWS, COLS))

def reference(inner, outer, momentum, residual):
    low = cosine_low()
    acc = outer[None] - inner.astype(jnp.float32) + residual
    blocks = acc.reshape(ISLANDS, ROWS // GROUP, GROUP, COLS // GROUP, GROUP)
    half = jnp.einsum('kn,irnbm->irkbm', low, blocks, precision=lax.Precision.HIGHEST)
    band = jnp.einsum('irkbm,lm->irkbl', half, low, precision=lax.Precision.HIGHEST)
    sent = invert(low, band)
    residual_next = acc - sent
    mean_band = lax.optimization_barrier(jnp.sum(band, axis=0)) / ISLANDS
    update = invert(low, mean_band)
    momentum_next = momentum_keep * momentum + update
    outer_next = outer - outer_rate * (update + momentum_keep * momentum_next)
    return (outer_next, momentum_next, residual_next)
```

```python
import functools

import jax
import jax.numpy as jnp
import ml_dtypes
import numpy as np
from jax import lax
from jax.experimental import pallas as pl
from jax.experimental.pallas import tpu as pltpu
from jax.sharding import PartitionSpec as P

GROUP = 128
BAND = 32
ROWS_DEV = 48
RING = 8
OUTER_RATE = 0.7
KEEP = 0.9
MESH = pl.DeviceIdType.MESH
BF16 = ml_dtypes.bfloat16


def split_np(a):
    hi = a.astype(np.float32).astype(BF16)
    lo = (a - hi.astype(np.float64)).astype(np.float32).astype(BF16)
    return hi, lo


def cosine_low():
    freq = np.arange(BAND, dtype=np.float64)[:, None]
    place = np.arange(GROUP, dtype=np.float64)[None, :]
    table = np.cos(np.pi * (2.0 * place + 1.0) * freq / (2.0 * GROUP))
    scale = np.where(freq == 0, np.sqrt(1.0 / GROUP), np.sqrt(2.0 / GROUP))
    return table * scale


def tables():
    low = cosine_low()
    diag = np.zeros((4 * GROUP, 4 * BAND))
    for q in range(4):
        diag[q * GROUP : (q + 1) * GROUP, q * BAND : (q + 1) * BAND] = low.T
    hi, lo = split_np(diag)
    col_fwd = np.concatenate([hi, lo], axis=1)
    hi, lo = split_np(diag.T)
    col_inv = np.concatenate([hi, hi, lo], axis=0)
    row_fwd = np.zeros((RING, 2 * BAND, 3 * ROWS_DEV), BF16)
    row_inv = np.zeros((RING, ROWS_DEV, 3 * 2 * BAND), BF16)
    for d in range(RING):
        rows = d * ROWS_DEV + np.arange(ROWS_DEV)
        first, last = rows[0] // GROUP, rows[-1] // GROUP
        part = np.zeros((2 * BAND, ROWS_DEV))
        for slot, b in enumerate((first, last)):
            if slot == 1 and first == last:
                continue
            inside = rows // GROUP == b
            part[slot * BAND : (slot + 1) * BAND, inside] = low[:, rows[inside] % GROUP]
        hi, lo = split_np(part)
        row_fwd[d] = np.concatenate([hi, hi, lo], axis=1)
        hi, lo = split_np(part.T)
        row_inv[d] = np.concatenate([hi, hi, lo], axis=1)
    return col_fwd, col_inv, row_fwd, row_inv


def split(a):
    hi = a.astype(jnp.bfloat16)
    lo = (a - hi.astype(jnp.float32)).astype(jnp.bfloat16)
    return hi, lo


def dot(a, b):
    return jnp.dot(a, b, preferred_element_type=jnp.float32)


def kernel(
    ny, cols,
    inner_in, outer_in, mom_in, res_in, colf_in, coli_in, rowf_in, rowi_in,
    outer_out, mom_out, res_out,
    inner_v, outer_v, mom_v, res_v, colf, coli, rowf, rowi,
    part, from_a, sums, from_y, band, total, load_sem, out_sem,
    a_send, a_recv, y_send, y_recv, b_send, b_recv, t_send, t_recv,
):
    hc = cols * BAND // GROUP // 2
    i, f = lax.axis_index("island"), lax.axis_index("fsdp")
    y, xl = lax.div(i, 2), lax.rem(i, 2)
    d = lax.rem(f, RING)
    base = f - d
    lo_b, hi_b = lax.div(3 * d, 8), lax.div(3 * d + 2, 8)
    first = lambda b: lax.div(8 * b, 3)
    last = lambda b: lax.div(8 * b + 7, 3)
    own_b, half = lax.div(d, 3), lax.rem(d, 3)
    owner = half != 2
    two = lo_b != hi_b

    def at(yy, xx, dd):
        return (yy * 2 + xx, base + dd)

    bar = pltpu.get_barrier_semaphore()
    lo_d, hi_d = first(lo_b), last(hi_b)
    for k in range(-3, 4):
        for xr in range(2):
            if k == 0 and xr == 0:
                continue

            @pl.when((d + k >= lo_d) & (d + k <= hi_d))
            def _():
                pl.semaphore_signal(bar, 1, device_id=at(y, lax.rem(xl + xr, 2), d + k), device_id_type=MESH)

    for k in range(1, ny):
        pl.semaphore_signal(bar, 1, device_id=at(lax.rem(y + k, ny), xl, d), device_id_type=MESH)

    loads = [
        pltpu.make_async_copy(src, dst, load_sem.at[n])
        for n, (src, dst) in enumerate(
            [
                (inner_in.at[0], inner_v), (res_in.at[0], res_v), (outer_in, outer_v), (colf_in, colf), (rowf_in.at[d], rowf),
                (coli_in, coli), (rowi_in.at[d], rowi), (mom_in, mom_v),
            ]
        )
    ]
    for c in loads:
        c.start()

    @pl.when(own_b != 1)
    def _():
        from_a[6:8] = jnp.zeros((2, 16, hc), jnp.float32)

    @pl.when(jnp.logical_not(two))
    def _():
        band[BAND:] = jnp.zeros((BAND, 2 * hc), jnp.float32)
        total[BAND:] = jnp.zeros((BAND, 2 * hc), jnp.float32)

    for c in loads[:5]:
        c.wait()

    res_v[...] = outer_v[...] - inner_v[...].astype(jnp.float32) + res_v[...]
    chunks = cols // 512
    acc = jnp.concatenate([res_v[:, 512 * c : 512 * (c + 1)] for c in range(chunks)], axis=0)
    hi, lo = split(acc)
    prod = dot(hi, colf[...])
    tall = prod[:, :128] + prod[:, 128:] + dot(lo, colf[:, :128])
    wide = jnp.concatenate([tall[ROWS_DEV * c : ROWS_DEV * (c + 1)] for c in range(chunks)], axis=1)
    hi, lo = split(wide)
    part[...] = dot(rowf[...], jnp.concatenate([hi, lo, hi], axis=0))

    pl.semaphore_wait(bar, (hi_d - lo_d + 1) * 2 - 1 + ny - 1)

    def rows16(n):
        return pl.ds(pl.multiple_of(n * 16, 16), 16)

    def half_cols(xx):
        return pl.ds(pl.multiple_of(xx * hc, 128), hc)

    def a_copies(run):
        for slot, b in enumerate((lo_b, hi_b)):
            for h in range(2):
                for xr in range(2):
                    to_x = lax.rem(xl + xr, 2)
                    to_d = 3 * b + h
                    cond = jnp.logical_not((to_d == d) & (xr == 0)) if slot == 0 else two
                    n = slot * 4 + h * 2 + xr

                    @pl.when(cond)
                    def _():
                        run(
                            pltpu.make_async_remote_copy(
                                part.at[slot * BAND + 16 * h : slot * BAND + 16 * h + 16, half_cols(to_x)],
                                from_a.at[(d - first(b)) * 2 + xl],
                                a_send.at[n],
                                a_recv.at[(d - first(b)) * 2 + xl],
                                device_id=at(y, to_x, to_d),
                                device_id_type=MESH,
                            )
                        )

    a_copies(lambda c: c.start())

    me_a = (d - first(own_b)) * 2 + xl

    @pl.when(owner)
    def _():
        from_a[me_a] = part[rows16(half), half_cols(xl)]

    def dummy(ref, send, recv):
        return pltpu.make_async_remote_copy(ref, ref, send, recv, device_id=at(y, 1 - xl, d), device_id_type=MESH)

    @pl.when(owner)
    def _():
        for n in range(8):
            @pl.when((n != me_a) & (first(own_b) + n // 2 <= last(own_b)))
            def _():
                dummy(from_a.at[n], a_send.at[n], a_recv.at[n]).wait_recv()

        def add(x):
            return (from_a[x] + from_a[2 + x]) + (from_a[4 + x] + from_a[6 + x])

        mine, other = add(xl), add(1 - xl)
        sums[0] = mine
        sums[1] = other
        from_y[y] = mine + other

    def y_copies(run):
        for k in range(1, ny):
            run(
                pltpu.make_async_remote_copy(
                    from_y.at[y], from_y.at[y], y_send.at[k], y_recv.at[y],
                    device_id=at(lax.rem(y + k, ny), xl, d), device_id_type=MESH,
                )
            )

    def b_copies(run, src, dst, send, recv):
        for m in range(4):
            to_d = first(own_b) + m
            slot = own_b - lax.div(3 * to_d, 8)
            for xr in range(2):
                @pl.when((to_d <= last(own_b)) & jnp.logical_not((to_d == d) & (xr == 0)))
                def _():
                    run(
                        pltpu.make_async_remote_copy(
                            src(xr),
                            dst.at[rows16(slot * 2 + half), half_cols(xl)],
                            send.at[m * 2 + xr],
                            recv.at[slot * 4 + half * 2 + xl],
                            device_id=at(y, lax.rem(xl + xr, 2), to_d),
                            device_id_type=MESH,
                        )
                    )

    def b_wait(dst, send, recv):
        for slot in range(2):
            for h in range(2):
                for x in range(2):
                    n = slot * 4 + h * 2 + x
                    cond = two if slot == 1 else jnp.logical_not((3 * lo_b + h == d) & (x == xl))

                    @pl.when(cond)
                    def _():
                        dummy(
                            dst.at[slot * BAND + 16 * h : slot * BAND + 16 * h + 16, hc * x : hc * x + hc], send.at[n], recv.at[n]
                        ).wait_recv()

    @pl.when(owner)
    def _():
        y_copies(lambda c: c.start())
        b_copies(lambda c: c.start(), lambda xr: sums.at[xr], band, b_send, b_recv)
        band[rows16(half), half_cols(xl)] = sums[0]

    for c in loads[5:]:
        c.wait()

    def invert(coef):
        hi, lo = split(coef)
        wide = dot(rowi[...], jnp.concatenate([hi, lo, hi], axis=0))
        tall = jnp.concatenate([wide[:, 128 * c : 128 * (c + 1)] for c in range(chunks)], axis=0)
        hi, lo = split(tall)
        return dot(jnp.concatenate([hi, lo, hi], axis=1), coli[...])

    b_wait(band, b_send, b_recv)
    sent = invert(band[...])
    for c in range(chunks):
        at_c = slice(512 * c, 512 * (c + 1))
        res_v[:, at_c] = res_v[:, at_c] - sent[ROWS_DEV * c : ROWS_DEV * (c + 1)]
    res_write = pltpu.make_async_copy(res_v, res_out.at[0], out_sem.at[0])
    res_write.start()

    @pl.when(owner)
    def _():
        for k in range(1, ny):
            n = lax.rem(y + k, ny)
            dummy(from_y.at[n], y_send.at[k], y_recv.at[n]).wait_recv()
        whole = from_y[0]
        for n in range(1, ny):
            whole = whole + from_y[n]
        sums[2] = whole * (1.0 / (2 * ny))
        b_copies(lambda c: c.start(), lambda xr: sums.at[2], total, t_send, t_recv)
        total[rows16(half), half_cols(xl)] = sums[2]

    b_wait(total, t_send, t_recv)
    update = invert(total[...])
    for c in range(chunks):
        at_c = slice(512 * c, 512 * (c + 1))
        u = update[ROWS_DEV * c : ROWS_DEV * (c + 1)]
        m = KEEP * mom_v[:, at_c] + u
        mom_v[:, at_c] = m
        outer_v[:, at_c] = outer_v[:, at_c] - OUTER_RATE * (u + KEEP * m)
    writes = [
        pltpu.make_async_copy(mom_v, mom_out, out_sem.at[1]),
        pltpu.make_async_copy(outer_v, outer_out, out_sem.at[2]),
    ]
    for c in writes:
        c.start()
    a_copies(lambda c: c.wait_send())

    @pl.when(owner)
    def _():
        y_copies(lambda c: c.wait_send())
        b_copies(lambda c: c.wait_send(), lambda xr: sums.at[xr], band, b_send, b_recv)
        b_copies(lambda c: c.wait_send(), lambda xr: sums.at[2], total, t_send, t_recv)

    res_write.wait()
    for c in writes:
        c.wait()


def solution(mesh):
    ny = mesh.shape["island"] // 2
    col_fwd, col_inv, row_fwd, row_inv = tables()

    def per_device(inner, outer, momentum, residual):
        rows, cols = outer.shape
        hc = cols * BAND // GROUP // 2
        f32, bf16 = jnp.float32, jnp.bfloat16
        dma = pltpu.SemaphoreType.DMA
        return tuple(
            pl.pallas_call(
                functools.partial(kernel, ny, cols),
                name="outer_step",
                out_shape=[
                    jax.ShapeDtypeStruct((rows, cols), f32),
                    jax.ShapeDtypeStruct((rows, cols), f32),
                    jax.ShapeDtypeStruct((1, rows, cols), f32),
                ],
                in_specs=[pl.BlockSpec(memory_space=pltpu.HBM)] * 8,
                out_specs=[pl.BlockSpec(memory_space=pl.ANY)] * 3,
                scratch_shapes=[
                    pltpu.VMEM((rows, cols), bf16),
                    pltpu.VMEM((rows, cols), f32),
                    pltpu.VMEM((rows, cols), f32),
                    pltpu.VMEM((rows, cols), f32),
                    pltpu.VMEM(col_fwd.shape, bf16),
                    pltpu.VMEM(col_inv.shape, bf16),
                    pltpu.VMEM(row_fwd.shape[1:], bf16),
                    pltpu.VMEM(row_inv.shape[1:], bf16),
                    pltpu.VMEM((2 * BAND, 2 * hc), f32),
                    pltpu.VMEM((8, 16, hc), f32),
                    pltpu.VMEM((3, 16, hc), f32),
                    pltpu.VMEM((ny, 16, hc), f32),
                    pltpu.VMEM((2 * BAND, 2 * hc), f32),
                    pltpu.VMEM((2 * BAND, 2 * hc), f32),
                    dma((8,)), dma((3,)),
                    dma((8,)), dma((8,)), dma((ny,)), dma((ny,)), dma((8,)), dma((8,)), dma((8,)), dma((8,)),
                ],
                compiler_params=pltpu.CompilerParams(
                    collective_id=0, has_side_effects=True, vmem_limit_bytes=40 * 1024 * 1024
                ),
            )(
                inner, outer, momentum, residual,
                jnp.asarray(col_fwd), jnp.asarray(col_inv), jnp.asarray(row_fwd), jnp.asarray(row_inv),
            )
        )

    return jax.shard_map(
        per_device,
        mesh=mesh,
        in_specs=(P("island", "fsdp", None), P("fsdp", None), P("fsdp", None), P("island", "fsdp", None)),
        out_specs=(P("fsdp", None), P("fsdp", None), P("island", "fsdp", None)),
        check_vma=False,
    )
```

```python
import functools

import jax
import jax.numpy as jnp
import ml_dtypes
import numpy as np
from jax import lax
from jax.experimental import pallas as pl
from jax.experimental.pallas import tpu as pltpu
from jax.sharding import PartitionSpec as P

GROUP = 128
BAND = 32
ROWS_DEV = 48
RING = 8
OUTER_RATE = 0.7
KEEP = 0.9
MESH = pl.DeviceIdType.MESH
BF16 = ml_dtypes.bfloat16


def split_np(a):
    hi = a.astype(np.float32).astype(BF16)
    lo = (a - hi.astype(np.float64)).astype(np.float32).astype(BF16)
    return hi, lo


def cosine_low():
    freq = np.arange(BAND, dtype=np.float64)[:, None]
    place = np.arange(GROUP, dtype=np.float64)[None, :]
    table = np.cos(np.pi * (2.0 * place + 1.0) * freq / (2.0 * GROUP))
    scale = np.where(freq == 0, np.sqrt(1.0 / GROUP), np.sqrt(2.0 / GROUP))
    return table * scale


def tables():
    low = cosine_low()
    diag = np.zeros((4 * GROUP, 4 * BAND))
    for q in range(4):
        diag[q * GROUP : (q + 1) * GROUP, q * BAND : (q + 1) * BAND] = low.T
    hi, lo = split_np(diag)
    col_fwd = np.concatenate([hi, lo], axis=1)
    hi, lo = split_np(diag.T)
    col_inv = np.concatenate([hi, hi, lo], axis=0)
    row_fwd = np.zeros((RING, 2 * BAND, 3 * ROWS_DEV), BF16)
    row_inv = np.zeros((RING, ROWS_DEV, 3 * 2 * BAND), BF16)
    for d in range(RING):
        rows = d * ROWS_DEV + np.arange(ROWS_DEV)
        first, last = rows[0] // GROUP, rows[-1] // GROUP
        part = np.zeros((2 * BAND, ROWS_DEV))
        for slot, b in enumerate((first, last)):
            if slot == 1 and first == last:
                continue
            inside = rows // GROUP == b
            part[slot * BAND : (slot + 1) * BAND, inside] = low[:, rows[inside] % GROUP]
        hi, lo = split_np(part)
        row_fwd[d] = np.concatenate([hi, hi, lo], axis=1)
        hi, lo = split_np(part.T)
        row_inv[d] = np.concatenate([hi, hi, lo], axis=1)
    return col_fwd, col_inv, row_fwd, row_inv


def split(a):
    hi = a.astype(jnp.bfloat16)
    lo = (a - hi.astype(jnp.float32)).astype(jnp.bfloat16)
    return hi, lo


def dot(a, b):
    return jnp.dot(a, b, preferred_element_type=jnp.float32)


def invert(coef, rowi, coli):
    hi, lo = split(coef)
    wide = dot(rowi, jnp.concatenate([hi, lo, hi], axis=0))
    tall = jnp.concatenate([wide[:, 128 * c : 128 * (c + 1)] for c in range(wide.shape[1] // 128)], axis=0)
    hi, lo = split(tall)
    return dot(jnp.concatenate([hi, lo, hi], axis=1), coli)


def kernel(
    ny, cols,
    inner_in, outer_in, res_in, colf_in, coli_in, rowf_in, rowi_in,
    total, res_out,
    inner_v, outer_v, res_v, colf, coli, rowf, rowi,
    part, from_a, sums, from_y, band, load_sem, out_sem,
    a_send, a_recv, y_send, y_recv, b_send, b_recv, t_send, t_recv,
):
    hc = cols * BAND // GROUP // 2
    i, f = lax.axis_index("island"), lax.axis_index("fsdp")
    y, xl = lax.div(i, 2), lax.rem(i, 2)
    d = lax.rem(f, RING)
    base = f - d
    lo_b, hi_b = lax.div(3 * d, 8), lax.div(3 * d + 2, 8)
    first = lambda b: lax.div(8 * b, 3)
    last = lambda b: lax.div(8 * b + 7, 3)
    own_b, half = lax.div(d, 3), lax.rem(d, 3)
    owner = half != 2
    two = lo_b != hi_b

    def at(yy, xx, dd):
        return (yy * 2 + xx, base + dd)

    bar = pltpu.get_barrier_semaphore()
    lo_d, hi_d = first(lo_b), last(hi_b)
    for k in range(-3, 4):
        for xr in range(2):
            if k == 0 and xr == 0:
                continue

            @pl.when((d + k >= lo_d) & (d + k <= hi_d))
            def _():
                pl.semaphore_signal(bar, 1, device_id=at(y, lax.rem(xl + xr, 2), d + k), device_id_type=MESH)

    for k in range(1, ny):
        pl.semaphore_signal(bar, 1, device_id=at(lax.rem(y + k, ny), xl, d), device_id_type=MESH)

    loads = [
        pltpu.make_async_copy(src, dst, load_sem.at[n])
        for n, (src, dst) in enumerate(
            [
                (inner_in.at[0], inner_v), (res_in.at[0], res_v), (outer_in, outer_v), (colf_in, colf), (rowf_in.at[d], rowf),
                (coli_in, coli), (rowi_in.at[d], rowi),
            ]
        )
    ]
    for c in loads:
        c.start()

    @pl.when(own_b != 1)
    def _():
        from_a[6:8] = jnp.zeros((2, 16, hc), jnp.float32)

    @pl.when(jnp.logical_not(two))
    def _():
        band[BAND:] = jnp.zeros((BAND, 2 * hc), jnp.float32)

    for c in loads[:5]:
        c.wait()

    res_v[...] = outer_v[...] - inner_v[...].astype(jnp.float32) + res_v[...]
    chunks = cols // 512
    acc = jnp.concatenate([res_v[:, 512 * c : 512 * (c + 1)] for c in range(chunks)], axis=0)
    hi, lo = split(acc)
    prod = dot(hi, colf[...])
    tall = prod[:, :128] + prod[:, 128:] + dot(lo, colf[:, :128])
    wide = jnp.concatenate([tall[ROWS_DEV * c : ROWS_DEV * (c + 1)] for c in range(chunks)], axis=1)
    hi, lo = split(wide)
    part[...] = dot(rowf[...], jnp.concatenate([hi, lo, hi], axis=0))

    pl.semaphore_wait(bar, (hi_d - lo_d + 1) * 2 - 1 + ny - 1)

    def rows16(n):
        return pl.ds(pl.multiple_of(n * 16, 16), 16)

    def half_cols(xx):
        return pl.ds(pl.multiple_of(xx * hc, 128), hc)

    def a_copies(run):
        for slot, b in enumerate((lo_b, hi_b)):
            for h in range(2):
                for xr in range(2):
                    to_x = lax.rem(xl + xr, 2)
                    to_d = 3 * b + h
                    cond = jnp.logical_not((to_d == d) & (xr == 0)) if slot == 0 else two
                    n = slot * 4 + h * 2 + xr

                    @pl.when(cond)
                    def _():
                        run(
                            pltpu.make_async_remote_copy(
                                part.at[slot * BAND + 16 * h : slot * BAND + 16 * h + 16, half_cols(to_x)],
                                from_a.at[(d - first(b)) * 2 + xl],
                                a_send.at[n],
                                a_recv.at[(d - first(b)) * 2 + xl],
                                device_id=at(y, to_x, to_d),
                                device_id_type=MESH,
                            )
                        )

    a_copies(lambda c: c.start())

    me_a = (d - first(own_b)) * 2 + xl

    @pl.when(owner)
    def _():
        from_a[me_a] = part[rows16(half), half_cols(xl)]

    def dummy(ref, send, recv):
        return pltpu.make_async_remote_copy(ref, ref, send, recv, device_id=at(y, 1 - xl, d), device_id_type=MESH)

    @pl.when(owner)
    def _():
        for n in range(8):
            @pl.when((n != me_a) & (first(own_b) + n // 2 <= last(own_b)))
            def _():
                dummy(from_a.at[n], a_send.at[n], a_recv.at[n]).wait_recv()

        def add(x):
            return (from_a[x] + from_a[2 + x]) + (from_a[4 + x] + from_a[6 + x])

        mine, other = add(xl), add(1 - xl)
        sums[0] = mine
        sums[1] = other
        from_y[y] = mine + other

    def y_copies(run):
        for k in range(1, ny):
            run(
                pltpu.make_async_remote_copy(
                    from_y.at[y], from_y.at[y], y_send.at[k], y_recv.at[y],
                    device_id=at(lax.rem(y + k, ny), xl, d), device_id_type=MESH,
                )
            )

    def b_copies(run, src, dst, send, recv):
        for m in range(4):
            to_d = first(own_b) + m
            slot = own_b - lax.div(3 * to_d, 8)
            for xr in range(2):
                @pl.when((to_d <= last(own_b)) & jnp.logical_not((to_d == d) & (xr == 0)))
                def _():
                    run(
                        pltpu.make_async_remote_copy(
                            src(xr),
                            dst.at[rows16(slot * 2 + half), half_cols(xl)],
                            send.at[m * 2 + xr],
                            recv.at[slot * 4 + half * 2 + xl],
                            device_id=at(y, lax.rem(xl + xr, 2), to_d),
                            device_id_type=MESH,
                        )
                    )

    def b_wait(dst, send, recv):
        for slot in range(2):
            for h in range(2):
                for x in range(2):
                    n = slot * 4 + h * 2 + x
                    cond = two if slot == 1 else jnp.logical_not((3 * lo_b + h == d) & (x == xl))

                    @pl.when(cond)
                    def _():
                        dummy(
                            dst.at[slot * BAND + 16 * h : slot * BAND + 16 * h + 16, hc * x : hc * x + hc], send.at[n], recv.at[n]
                        ).wait_recv()

    @pl.when(owner)
    def _():
        y_copies(lambda c: c.start())
        b_copies(lambda c: c.start(), lambda xr: sums.at[xr], band, b_send, b_recv)
        band[rows16(half), half_cols(xl)] = sums[0]

    for c in loads[5:]:
        c.wait()

    b_wait(band, b_send, b_recv)
    sent = invert(band[...], rowi[...], coli[...])
    for c in range(chunks):
        at_c = slice(512 * c, 512 * (c + 1))
        res_v[:, at_c] = res_v[:, at_c] - sent[ROWS_DEV * c : ROWS_DEV * (c + 1)]
    res_write = pltpu.make_async_copy(res_v, res_out, out_sem.at[0])
    res_write.start()

    @pl.when(owner)
    def _():
        for k in range(1, ny):
            n = lax.rem(y + k, ny)
            dummy(from_y.at[n], y_send.at[k], y_recv.at[n]).wait_recv()
        whole = from_y[0]
        for n in range(1, ny):
            whole = whole + from_y[n]
        sums[2] = whole * (1.0 / (2 * ny))
        b_copies(lambda c: c.start(), lambda xr: sums.at[2], total, t_send, t_recv)
        mine = pltpu.make_async_copy(sums.at[2], total.at[rows16(half), half_cols(xl)], out_sem.at[1])
        mine.start()
        mine.wait()

    b_wait(total, t_send, t_recv)
    a_copies(lambda c: c.wait_send())

    @pl.when(owner)
    def _():
        y_copies(lambda c: c.wait_send())
        b_copies(lambda c: c.wait_send(), lambda xr: sums.at[xr], band, b_send, b_recv)
        b_copies(lambda c: c.wait_send(), lambda xr: sums.at[2], total, t_send, t_recv)

    res_write.wait()


def finish(
    cols,
    total_in, res_in, outer_in, mom_in, coli_in, rowi_in,
    outer_out, mom_out, res_out,
    total, outer_v, mom_v, coli, rowi, load_sem, out_sem,
):
    d = lax.rem(lax.axis_index("fsdp"), RING)
    two = lax.div(3 * d, 8) != lax.div(3 * d + 2, 8)
    writes = [
        pltpu.make_async_copy(src, dst, out_sem.at[n])
        for n, (src, dst) in enumerate([(res_in, res_out.at[0]), (mom_v, mom_out), (outer_v, outer_out)])
    ]
    loads = [
        pltpu.make_async_copy(src, dst, load_sem.at[n])
        for n, (src, dst) in enumerate(
            [(total_in, total), (rowi_in.at[d], rowi), (coli_in, coli), (mom_in, mom_v), (outer_in, outer_v)]
        )
    ]
    for c in loads:
        c.start()
    writes[0].start()
    loads[0].wait()

    @pl.when(jnp.logical_not(two))
    def _():
        total[BAND:] = jnp.zeros((BAND, cols * BAND // GROUP), jnp.float32)

    for c in loads[1:]:
        c.wait()
    update = invert(total[...], rowi[...], coli[...])
    for c in range(cols // 512):
        at_c = slice(512 * c, 512 * (c + 1))
        u = update[ROWS_DEV * c : ROWS_DEV * (c + 1)]
        m = KEEP * mom_v[:, at_c] + u
        mom_v[:, at_c] = m
        outer_v[:, at_c] = outer_v[:, at_c] - OUTER_RATE * (u + KEEP * m)
    for c in writes[1:]:
        c.start()
    for c in writes:
        c.wait()


def solution(mesh):
    ny = mesh.shape["island"] // 2
    col_fwd, col_inv, row_fwd, row_inv = tables()

    def per_device(inner, outer, momentum, residual):
        rows, cols = outer.shape
        hc = cols * BAND // GROUP // 2
        f32, bf16 = jnp.float32, jnp.bfloat16
        dma = pltpu.SemaphoreType.DMA
        any_space = pl.BlockSpec(memory_space=pl.ANY)
        in_hbm = lambda a: pltpu.with_memory_space_constraint(a, pltpu.HBM)
        colf, coli, rowf, rowi = (jnp.asarray(a) for a in (col_fwd, col_inv, row_fwd, row_inv))
        total, res_next = pl.pallas_call(
            functools.partial(kernel, ny, cols),
            name="exchange",
            out_shape=[pltpu.VMEM((2 * BAND, 2 * hc), f32), pltpu.VMEM((rows, cols), f32)],
            in_specs=[any_space] * 7,
            out_specs=[any_space] * 2,
            scratch_shapes=[
                pltpu.VMEM((rows, cols), bf16),
                pltpu.VMEM((rows, cols), f32),
                pltpu.VMEM((rows, cols), f32),
                pltpu.VMEM(col_fwd.shape, bf16),
                pltpu.VMEM(col_inv.shape, bf16),
                pltpu.VMEM(row_fwd.shape[1:], bf16),
                pltpu.VMEM(row_inv.shape[1:], bf16),
                pltpu.VMEM((2 * BAND, 2 * hc), f32),
                pltpu.VMEM((8, 16, hc), f32),
                pltpu.VMEM((3, 16, hc), f32),
                pltpu.VMEM((ny, 16, hc), f32),
                pltpu.VMEM((2 * BAND, 2 * hc), f32),
                dma((7,)), dma((2,)),
                dma((8,)), dma((8,)), dma((ny,)), dma((ny,)), dma((8,)), dma((8,)), dma((8,)), dma((8,)),
            ],
            compiler_params=pltpu.CompilerParams(
                collective_id=0, has_side_effects=True, vmem_limit_bytes=24 * 1024 * 1024
            ),
        )(*map(in_hbm, (inner, outer, residual, colf, coli, rowf, rowi)))
        return tuple(
            pl.pallas_call(
                functools.partial(finish, cols),
                name="finish",
                out_shape=[
                    jax.ShapeDtypeStruct((rows, cols), f32),
                    jax.ShapeDtypeStruct((rows, cols), f32),
                    jax.ShapeDtypeStruct((1, rows, cols), f32),
                ],
                in_specs=[any_space] * 6,
                out_specs=[any_space] * 3,
                scratch_shapes=[
                    pltpu.VMEM((2 * BAND, 2 * hc), f32),
                    pltpu.VMEM((rows, cols), f32),
                    pltpu.VMEM((rows, cols), f32),
                    pltpu.VMEM(col_inv.shape, bf16),
                    pltpu.VMEM(row_inv.shape[1:], bf16),
                    dma((5,)), dma((3,)),
                ],
                compiler_params=pltpu.CompilerParams(vmem_limit_bytes=24 * 1024 * 1024),
            )(total, res_next, outer, momentum, coli, rowi)
        )

    return jax.shard_map(
        per_device,
        mesh=mesh,
        in_specs=(P("island", "fsdp", None), P("fsdp", None), P("fsdp", None), P("island", "fsdp", None)),
        out_specs=(P("fsdp", None), P("fsdp", None), P("island", "fsdp", None)),
        check_vma=False,
    )
```

```python
import functools

import jax
import jax.numpy as jnp
import ml_dtypes
import numpy as np
from jax import lax
from jax.experimental import pallas as pl
from jax.experimental.pallas import tpu as pltpu
from jax.sharding import PartitionSpec as P

GROUP = 128
BAND = 32
ROWS_DEV = 48
RING = 8
OUTER_RATE = 0.7
KEEP = 0.9
MESH = pl.DeviceIdType.MESH
BF16 = ml_dtypes.bfloat16


def split_np(a):
    hi = a.astype(np.float32).astype(BF16)
    lo = (a - hi.astype(np.float64)).astype(np.float32).astype(BF16)
    return hi, lo


def cosine_low():
    freq = np.arange(BAND, dtype=np.float64)[:, None]
    place = np.arange(GROUP, dtype=np.float64)[None, :]
    table = np.cos(np.pi * (2.0 * place + 1.0) * freq / (2.0 * GROUP))
    scale = np.where(freq == 0, np.sqrt(1.0 / GROUP), np.sqrt(2.0 / GROUP))
    return table * scale


def tables():
    low = cosine_low()
    diag = np.zeros((4 * GROUP, 4 * BAND))
    for q in range(4):
        diag[q * GROUP : (q + 1) * GROUP, q * BAND : (q + 1) * BAND] = low.T
    hi, lo = split_np(diag)
    col_fwd = np.concatenate([hi, lo], axis=1)
    hi, lo = split_np(diag.T)
    col_inv = np.concatenate([hi, hi, lo], axis=0)
    row_fwd = np.zeros((RING, 2 * BAND, 3 * ROWS_DEV), BF16)
    row_inv = np.zeros((RING, ROWS_DEV, 3 * 2 * BAND), BF16)
    for d in range(RING):
        rows = d * ROWS_DEV + np.arange(ROWS_DEV)
        first, last = rows[0] // GROUP, rows[-1] // GROUP
        part = np.zeros((2 * BAND, ROWS_DEV))
        for slot, b in enumerate((first, last)):
            if slot == 1 and first == last:
                continue
            inside = rows // GROUP == b
            part[slot * BAND : (slot + 1) * BAND, inside] = low[:, rows[inside] % GROUP]
        hi, lo = split_np(part)
        row_fwd[d] = np.concatenate([hi, hi, lo], axis=1)
        hi, lo = split_np(part.T)
        row_inv[d] = np.concatenate([hi, hi, lo], axis=1)
    return col_fwd, col_inv, row_fwd, row_inv


def split(a):
    hi = a.astype(jnp.bfloat16)
    lo = (a - hi.astype(jnp.float32)).astype(jnp.bfloat16)
    return hi, lo


def dot(a, b):
    return jnp.dot(a, b, preferred_element_type=jnp.float32)


def invert(coef, rowi, coli):
    hi, lo = split(coef)
    wide = dot(rowi, jnp.concatenate([hi, lo, hi], axis=0))
    tall = jnp.concatenate([wide[:, 128 * c : 128 * (c + 1)] for c in range(wide.shape[1] // 128)], axis=0)
    hi, lo = split(tall)
    return dot(jnp.concatenate([hi, lo, hi], axis=1), coli)


def kernel(
    ny, cols,
    inner_in, outer_in, mom_in, res_in, colf_in, coli_in, rowf_in, rowi_in,
    total, res, outer, mom, coli, rowi,
    inner, colf, rowf, part, from_a, sums, from_y, band,
    load_sem, own_sem, up_sem, ring_sem,
    a_send, a_recv, y_send, y_recv, b_send, b_recv, t_send, t_recv,
):
    hc = cols * BAND // GROUP // 2
    wide = cols // 2
    i, f = lax.axis_index("island"), lax.axis_index("fsdp")
    y, xl = lax.div(i, 2), lax.rem(i, 2)
    d = lax.rem(f, RING)
    base = f - d
    lo_b, hi_b = lax.div(3 * d, 8), lax.div(3 * d + 2, 8)
    first = lambda b: lax.div(8 * b, 3)
    last = lambda b: lax.div(8 * b + 7, 3)
    own_b, half = lax.div(d, 3), lax.rem(d, 3)
    owner = half != 2
    two = lo_b != hi_b
    prim = jnp.where(d == RING - 3, 1, 0)
    prim_b = jnp.where(prim == 1, hi_b, lo_b)

    def at(yy, xx, dd):
        return (yy * 2 + xx, base + dd)

    def signal(sem, where):
        pl.semaphore_signal(sem, 1, device_id=where, device_id_type=MESH)

    def half_of(r):
        return lax.rem(xl + 1 + r, 2)

    def wide_cols(r):
        return pl.ds(pl.multiple_of(half_of(r) * wide, 128), wide)

    loads = []

    def load(src, dst):
        loads.append(pltpu.make_async_copy(src, dst, load_sem.at[len(loads)]))
        loads[-1].start()

    load(inner_in.at[0, :, wide_cols(0)], inner.at[0])
    load(res_in.at[0, :, wide_cols(0)], res.at[0])
    load(outer_in.at[:, wide_cols(0)], outer.at[0])
    load(colf_in, colf)

    bar = pltpu.get_barrier_semaphore()
    x2 = 1 - xl
    for m in range(3):
        to_d = jnp.where(prim_b == 1, 3 + m, first(prim_b) + m)
        for xr in range(2):
            @pl.when(((to_d != d) | (xr == 1)) & ((prim_b != 1) | (m < 2)))
            def _():
                signal(bar, at(y, lax.rem(xl + xr, 2), to_d))

    @pl.when(two)
    def _():
        for m in range(2):
            for xr in range(2):
                signal(bar, at(y, lax.rem(xl + xr, 2), 3 + m))

    @pl.when(owner)
    def _():
        for k in (1, 2, ny - 1, ny - 2):
            signal(bar, at(lax.rem(y + k, ny), xl, d))

    load(inner_in.at[0, :, wide_cols(1)], inner.at[1])
    load(res_in.at[0, :, wide_cols(1)], res.at[1])
    load(outer_in.at[:, wide_cols(1)], outer.at[1])
    load(rowf_in.at[d], rowf)

    @pl.when(own_b != 1)
    def _():
        from_a[6:8] = jnp.zeros((2, 16, hc), jnp.float32)

    @pl.when(jnp.logical_not(two))
    def _():
        band[:, BAND:] = jnp.zeros((2, BAND, hc), jnp.float32)
        total[BAND:] = jnp.zeros((BAND, 2 * hc), jnp.float32)

    chunks = wide // 512

    def forward(r):
        acc = outer[r] - inner[r].astype(jnp.float32) + res[r]
        res[r] = acc
        hi, lo = split(jnp.concatenate([acc[:, 512 * c : 512 * (c + 1)] for c in range(chunks)], axis=0))
        prod = dot(hi, colf[...])
        tall = prod[:, :128] + prod[:, 128:] + dot(lo, colf[:, :128])
        hi, lo = split(jnp.concatenate([tall[ROWS_DEV * c : ROWS_DEV * (c + 1)] for c in range(chunks)], axis=1))
        part[r] = dot(rowf[...], jnp.concatenate([hi, lo, hi], axis=0))

    def rows16(n):
        return pl.ds(pl.multiple_of(n * 16, 16), 16)

    def half_cols(xx):
        return pl.ds(pl.multiple_of(xx * hc, 128), hc)

    def a_copies(run, r, second):
        slot = 1 - prim if second else prim
        b = 1 if second else prim_b
        for h in range(2):
            to_d = 3 * b + h

            def go():
                run(
                    pltpu.make_async_remote_copy(
                        part.at[r, rows16(slot * 2 + h)],
                        from_a.at[(d - first(b)) * 2 + xl],
                        a_send.at[second * 4 + h * 2 + r],
                        a_recv.at[(d - first(b)) * 2 + xl],
                        device_id=at(y, half_of(r), to_d),
                        device_id_type=MESH,
                    )
                )

            if second or r == 0:
                go()
            else:
                pl.when(to_d != d)(go)

    for c in loads[:4]:
        c.wait()
    loads[7].wait()
    forward(0)
    pl.semaphore_wait(bar, jnp.where(two, 5, jnp.where(own_b == 1, 11, 9)))

    a_copies(lambda c: c.start(), 0, False)

    @pl.when((d == 3) | (d == 4))
    def _():
        signal(up_sem, at(y, xl, jnp.where(d == 3, 2, 5)))

    @pl.when(owner)
    def _():
        for k in (2, ny - 2):
            signal(ring_sem, at(lax.rem(y + k, ny), xl, d))

    for c in loads[4:7]:
        c.wait()
    forward(1)
    a_copies(lambda c: c.start(), 1, False)

    @pl.when(two)
    def _():
        pl.semaphore_wait(up_sem, 1)
        a_copies(lambda c: c.start(), 0, True)
        a_copies(lambda c: c.start(), 1, True)

    load(coli_in, coli)
    load(rowi_in.at[d], rowi)
    load(mom_in, mom)

    me_a = (d - first(own_b)) * 2 + xl

    def dummy(ref, send, recv):
        return pltpu.make_async_remote_copy(ref, ref, send, recv, device_id=at(y, x2, d), device_id_type=MESH)

    def y_copies(run):
        for k in (4, 3, 5, 2, 6, 1, 7):
            run(
                pltpu.make_async_remote_copy(
                    from_y.at[y], from_y.at[y], y_send.at[k], y_recv.at[y],
                    device_id=at(lax.rem(y + k, ny), xl, d), device_id_type=MESH,
                )
            )

    def b_copies(run, src, dst, send, recv):
        for m in range(4):
            to_d = first(own_b) + m
            slot = own_b - lax.div(3 * to_d, 8)
            for xr in range(2):
                @pl.when((to_d <= last(own_b)) & ((to_d != d) | (xr == 1)))
                def _():
                    run(
                        pltpu.make_async_remote_copy(
                            src(xr),
                            dst(slot * 2 + half, xr),
                            send.at[m * 2 + xr],
                            recv.at[slot * 4 + half * 2 + 1 - xr],
                            device_id=at(y, lax.rem(xl + xr, 2), to_d),
                            device_id_type=MESH,
                        )
                    )

    def b_wait(send, recv):
        for slot in range(2):
            for h in range(2):
                for r in range(2):
                    n = slot * 4 + h * 2 + r

                    @pl.when(two if slot == 1 else ((3 * lo_b + h != d) | (r == 0)))
                    def _():
                        dummy(sums.at[0], send.at[n], recv.at[n]).wait_recv()

    band_at = lambda n, xr: band.at[1 - xr, rows16(n)]
    total_at = lambda n, xr: total.at[rows16(n), half_cols(xl)]

    @pl.when(owner)
    def _():
        from_a[me_a] = part[1, rows16(half)]
        for n in range(8):
            @pl.when((n != me_a) & (first(own_b) + n // 2 <= last(own_b)))
            def _():
                dummy(from_a.at[n], a_send.at[n], a_recv.at[n]).wait_recv()

        def add(x):
            return (from_a[x] + from_a[2 + x]) + (from_a[4 + x] + from_a[6 + x])

        mine, other = add(xl), add(1 - xl)
        sums[0] = mine
        sums[1] = other
        from_y[y] = mine + other
        pl.semaphore_wait(ring_sem, 2)
        y_copies(lambda c: c.start())
        b_copies(lambda c: c.start(), lambda xr: sums.at[xr], band_at, b_send, b_recv)
        band[1, rows16(half)] = mine

    for c in loads[8:]:
        c.wait()

    b_wait(b_send, b_recv)
    sent = invert(jnp.concatenate([band[0], band[1]], axis=1), rowi[...], coli[...])
    for c in range(2 * chunks):
        r, at_c = c // chunks, slice(512 * (c % chunks), 512 * (c % chunks + 1))
        res[r, :, at_c] = res[r, :, at_c] - sent[ROWS_DEV * c : ROWS_DEV * (c + 1)]

    @pl.when(owner)
    def _():
        for k in range(1, ny):
            n = lax.rem(y + k, ny)
            dummy(from_y.at[n], y_send.at[k], y_recv.at[n]).wait_recv()
        whole = from_y[0]
        for n in range(1, ny):
            whole = whole + from_y[n]
        sums[2] = whole * (1.0 / (2 * ny))
        b_copies(lambda c: c.start(), lambda xr: sums.at[2], total_at, t_send, t_recv)
        total[rows16(half), half_cols(xl)] = sums[2]

    for r in range(2):
        a_copies(lambda c: c.wait_send(), r, False)

    @pl.when(two)
    def _():
        for r in range(2):
            a_copies(lambda c: c.wait_send(), r, True)

    @pl.when(owner)
    def _():
        y_copies(lambda c: c.wait_send())
        b_copies(lambda c: c.wait_send(), lambda xr: sums.at[xr], band_at, b_send, b_recv)

    b_wait(t_send, t_recv)

    @pl.when(owner)
    def _():
        b_copies(lambda c: c.wait_send(), lambda xr: sums.at[2], total_at, t_send, t_recv)


def finish(
    cols,
    total, res, outer, mom, coli, rowi,
    outer_out, mom_out, res_out,
    outer_v, mom_v, out_sem,
):
    xl = lax.rem(lax.axis_index("island"), 2)
    wide = cols // 2
    writes = []

    def write(src, dst):
        writes.append(pltpu.make_async_copy(src, dst, out_sem.at[len(writes)]))
        writes[-1].start()

    def columns(r, n, width):
        return pl.ds(pl.multiple_of(lax.rem(xl + 1 + r, 2) * wide + n, 128), width)

    for r in range(2):
        write(res.at[r], res_out.at[0, :, columns(r, 0, wide)])
    hi, lo = split(total[...])
    half = dot(rowi[...], jnp.concatenate([hi, lo, hi], axis=0))
    step = 1024
    for c in range(cols // step):
        at_c = slice(step * c, step * (c + 1))
        tall = jnp.concatenate([half[:, 128 * q : 128 * (q + 1)] for q in range(c * step // 512, (c + 1) * step // 512)], axis=0)
        hi, lo = split(tall)
        update = dot(jnp.concatenate([hi, lo, hi], axis=1), coli[...])
        for q in range(step // 512):
            n = (c * step + 512 * q) % wide
            r = (c * step + 512 * q) // wide
            at_q = slice(step * c + 512 * q, step * c + 512 * (q + 1))
            u = update[ROWS_DEV * q : ROWS_DEV * (q + 1)]
            rel = jnp.where(r == xl, 1, 0)
            m = KEEP * mom[:, at_q] + u
            mom_v[:, at_q] = m
            outer_v[:, at_q] = outer[rel, :, n : n + 512] - OUTER_RATE * (u + KEEP * m)
        write(mom_v.at[:, at_c], mom_out.at[:, at_c])
        write(outer_v.at[:, at_c], outer_out.at[:, at_c])
    for c in writes:
        c.wait()


def solution(mesh):
    ny = mesh.shape["island"] // 2
    col_fwd, col_inv, row_fwd, row_inv = tables()

    def per_device(inner, outer, momentum, residual):
        rows, cols = outer.shape
        hc = cols * BAND // GROUP // 2
        f32, bf16 = jnp.float32, jnp.bfloat16
        dma, regular = pltpu.SemaphoreType.DMA, pltpu.SemaphoreType.REGULAR
        any_space = pl.BlockSpec(memory_space=pl.ANY)
        vmem = pl.BlockSpec(memory_space=pltpu.VMEM)
        in_hbm = lambda a: pltpu.with_memory_space_constraint(a, pltpu.HBM)
        tables_hbm = [jnp.asarray(a) for a in (col_fwd, col_inv, row_fwd, row_inv)]
        passed = pl.pallas_call(
            functools.partial(kernel, ny, cols),
            name="exchange",
            out_shape=[
                pltpu.VMEM((2 * BAND, 2 * hc), f32),
                pltpu.VMEM((2, rows, cols // 2), f32),
                pltpu.VMEM((2, rows, cols // 2), f32),
                pltpu.VMEM((rows, cols), f32),
                pltpu.VMEM(col_inv.shape, bf16),
                pltpu.VMEM(row_inv.shape[1:], bf16),
            ],
            in_specs=[any_space] * 8,
            out_specs=[vmem] * 6,
            scratch_shapes=[
                pltpu.VMEM((2, rows, cols // 2), bf16),
                pltpu.VMEM(col_fwd.shape, bf16),
                pltpu.VMEM(row_fwd.shape[1:], bf16),
                pltpu.VMEM((2, 2 * BAND, hc), f32),
                pltpu.VMEM((8, 16, hc), f32),
                pltpu.VMEM((3, 16, hc), f32),
                pltpu.VMEM((ny, 16, hc), f32),
                pltpu.VMEM((2, 2 * BAND, hc), f32),
                dma((11,)), dma((1,)), regular, regular,
                dma((8,)), dma((8,)), dma((ny,)), dma((ny,)), dma((8,)), dma((8,)), dma((8,)), dma((8,)),
            ],
            compiler_params=pltpu.CompilerParams(
                collective_id=0, has_side_effects=True, vmem_limit_bytes=24 * 1024 * 1024
            ),
        )(*map(in_hbm, (inner, outer, momentum, residual, *tables_hbm)))
        return tuple(
            pl.pallas_call(
                functools.partial(finish, cols),
                name="finish",
                out_shape=[
                    jax.ShapeDtypeStruct((rows, cols), f32),
                    jax.ShapeDtypeStruct((rows, cols), f32),
                    jax.ShapeDtypeStruct((1, rows, cols), f32),
                ],
                in_specs=[vmem] * 6,
                out_specs=[any_space] * 3,
                scratch_shapes=[pltpu.VMEM((rows, cols), f32), pltpu.VMEM((rows, cols), f32), dma((8,))],
                compiler_params=pltpu.CompilerParams(vmem_limit_bytes=24 * 1024 * 1024),
            )(*passed)
        )

    return jax.shard_map(
        per_device,
        mesh=mesh,
        in_specs=(P("island", "fsdp", None), P("fsdp", None), P("fsdp", None), P("island", "fsdp", None)),
        out_specs=(P("fsdp", None), P("fsdp", None), P("island", "fsdp", None)),
        check_vma=False,
    )
```

```python
import functools

import jax
import jax.numpy as jnp
import ml_dtypes
import numpy as np
from jax import lax
from jax.experimental import pallas as pl
from jax.experimental.pallas import tpu as pltpu
from jax.sharding import PartitionSpec as P

GROUP = 128
BAND = 32
ROWS_DEV = 48
RING = 8
OUTER_RATE = 0.7
KEEP = 0.9
MESH = pl.DeviceIdType.MESH
BF16 = ml_dtypes.bfloat16


def split_np(a):
    hi = a.astype(np.float32).astype(BF16)
    lo = (a - hi.astype(np.float64)).astype(np.float32).astype(BF16)
    return hi, lo


def cosine_low():
    freq = np.arange(BAND, dtype=np.float64)[:, None]
    place = np.arange(GROUP, dtype=np.float64)[None, :]
    table = np.cos(np.pi * (2.0 * place + 1.0) * freq / (2.0 * GROUP))
    scale = np.where(freq == 0, np.sqrt(1.0 / GROUP), np.sqrt(2.0 / GROUP))
    return table * scale


def tables():
    low = cosine_low()
    diag = np.zeros((4 * GROUP, 4 * BAND))
    for q in range(4):
        diag[q * GROUP : (q + 1) * GROUP, q * BAND : (q + 1) * BAND] = low.T
    hi, lo = split_np(diag)
    col_fwd = np.concatenate([hi, lo], axis=1)
    hi, lo = split_np(diag.T)
    col_inv = np.concatenate([hi, hi, lo], axis=0)
    row_fwd = np.zeros((RING, 2 * BAND, 3 * ROWS_DEV), BF16)
    row_inv = np.zeros((RING, ROWS_DEV, 3 * 2 * BAND), BF16)
    for d in range(RING):
        rows = d * ROWS_DEV + np.arange(ROWS_DEV)
        first, last = rows[0] // GROUP, rows[-1] // GROUP
        part = np.zeros((2 * BAND, ROWS_DEV))
        for slot, b in enumerate((first, last)):
            if slot == 1 and first == last:
                continue
            inside = rows // GROUP == b
            part[slot * BAND : (slot + 1) * BAND, inside] = low[:, rows[inside] % GROUP]
        hi, lo = split_np(part)
        row_fwd[d] = np.concatenate([hi, hi, lo], axis=1)
        hi, lo = split_np(part.T)
        row_inv[d] = np.concatenate([hi, hi, lo], axis=1)
    return col_fwd, col_inv, row_fwd, row_inv


def split(a):
    hi = a.astype(jnp.bfloat16)
    lo = (a - hi.astype(jnp.float32)).astype(jnp.bfloat16)
    return hi, lo


def dot(a, b):
    return jnp.dot(a, b, preferred_element_type=jnp.float32)


def invert(coef, rowi, coli):
    hi, lo = split(coef)
    wide = dot(rowi, jnp.concatenate([hi, lo, hi], axis=0))
    tall = jnp.concatenate([wide[:, 128 * c : 128 * (c + 1)] for c in range(wide.shape[1] // 128)], axis=0)
    hi, lo = split(tall)
    return dot(jnp.concatenate([hi, lo, hi], axis=1), coli)


OWNS = {1: (0, 0, 24), 2: (0, 24, 8), 3: (1, 0, 16), 4: (1, 16, 16), 5: (2, 0, 8), 6: (2, 8, 24)}
MEMBERS = ((0, 1, 2), (2, 3, 4, 5), (5, 6, 7))
MOST = 24


def blocks_of(d):
    return [b for b in range(3) if d in MEMBERS[b]]


def owners_of(b):
    return [d for d in OWNS if OWNS[d][0] == b]


def kernel(
    ny, cols,
    inner_in, outer_in, mom_in, res_in, colf_in, coli_in, rowf_in, rowi_in,
    total, res, outer, mom, coli, rowi,
    inner, colf, rowf, part, from_a, sums, from_y, band,
    load_sem, up_sem, ring_sem,
    a_send, a_recv, y_send, y_recv, b_send, b_recv, t_send, t_recv,
):
    hc = cols * BAND // GROUP // 2
    wide = cols // 2
    i, f = lax.axis_index("island"), lax.axis_index("fsdp")
    y, xl = lax.div(i, 2), lax.rem(i, 2)
    d = lax.rem(f, RING)
    base = f - d

    def at(yy, xr, dd):
        return (yy * 2 + (1 - xl if xr else xl), base + dd)

    def ring(k):
        return lax.rem(y + k, ny)

    def signal(sem, where):
        pl.semaphore_signal(sem, 1, device_id=where, device_id_type=MESH)

    def each(devices, body):
        for dd in devices:
            pl.when(d == dd)(functools.partial(body, dd))

    def wide_cols(r):
        return pl.ds(pl.multiple_of((xl if r else 1 - xl) * wide, 128), wide)

    loads = []

    def load(src, dst):
        loads.append(pltpu.make_async_copy(src, dst, load_sem.at[len(loads)]))
        loads[-1].start()

    load(inner_in.at[0, :, wide_cols(0)], inner.at[0])
    load(res_in.at[0, :, wide_cols(0)], res.at[0])
    load(outer_in.at[:, wide_cols(0)], outer.at[0])
    load(colf_in, colf)

    bar = pltpu.get_barrier_semaphore()

    def greet(dd):
        for m in MEMBERS[OWNS[dd][0]]:
            if OWNS[dd][0] == 1 and m in (2, 5):
                continue
            for xr in range(2):
                if (m, xr) != (dd, 0):
                    signal(bar, at(y, xr, m))
        if dd in (2, 5):
            signal(bar, at(y, 0, 3 if dd == 2 else 4))
        for k in (1, ny - 1, 2, ny - 2):
            signal(bar, at(ring(k), 0, dd))

    each(OWNS, greet)

    load(inner_in.at[0, :, wide_cols(1)], inner.at[1])
    load(res_in.at[0, :, wide_cols(1)], res.at[1])
    load(outer_in.at[:, wide_cols(1)], outer.at[1])
    load(rowf_in.at[d], rowf)

    @pl.when((d != 2) & (d != 5))
    def _():
        band[:, BAND:] = jnp.zeros((2, BAND, hc), jnp.float32)
        total[BAND:] = jnp.zeros((BAND, 2 * hc), jnp.float32)

    chunks = wide // 512

    def forward(r):
        acc = outer[r] - inner[r].astype(jnp.float32) + res[r]
        res[r] = acc
        hi, lo = split(jnp.concatenate([acc[:, 512 * c : 512 * (c + 1)] for c in range(chunks)], axis=0))
        prod = dot(hi, colf[...])
        tall = prod[:, :128] + prod[:, 128:] + dot(lo, colf[:, :128])
        hi, lo = split(jnp.concatenate([tall[ROWS_DEV * c : ROWS_DEV * (c + 1)] for c in range(chunks)], axis=1))
        part[r] = dot(rowf[...], jnp.concatenate([hi, lo, hi], axis=0))

    def half_cols():
        return pl.ds(pl.multiple_of(xl * hc, 128), hc)

    def wait_rows(send, recv, rows, count=1):
        ref = part.at[0, :rows] if count == 1 else from_a.at[:count, :rows]
        sems = (send, send) if recv is None else (recv, recv)
        copy = pltpu.make_async_remote_copy(ref, ref, *sems, device_id=at(y, 1, d), device_id_type=MESH)
        copy.wait_recv() if recv is not None else copy.wait_send()

    def a_send_half(dd, r, b):
        slot = blocks_of(dd).index(b)
        for to in owners_of(b):
            if (to, r) == (dd, 1):
                continue
            row, rows = OWNS[to][1:]
            pltpu.make_async_remote_copy(
                part.at[r, slot * BAND + row : slot * BAND + row + rows],
                from_a.at[MEMBERS[b].index(dd) * 2 + 1 - r, :rows],
                a_send,
                a_recv,
                device_id=at(y, 1 - r, to),
                device_id_type=MESH,
            ).start()

    def first_block(dd):
        return 2 if dd == 5 else blocks_of(dd)[0]

    for c in loads[:4]:
        c.wait()
    loads[7].wait()
    forward(0)
    pl.semaphore_wait(bar, jnp.where((d == 0) | (d == 7), 4, jnp.where((d == 3) | (d == 4), 8, 7)))
    each(range(RING), lambda dd: a_send_half(dd, 0, first_block(dd)))

    @pl.when((d == 3) | (d == 4))
    def _():
        signal(up_sem, at(y, 0, jnp.where(d == 3, 2, 5)))

    @pl.when((d != 0) & (d != 7))
    def _():
        for k in (2, ny - 2):
            signal(ring_sem, at(ring(k), 0, d))

    for c in loads[4:7]:
        c.wait()
    forward(1)

    def a_rest(dd):
        a_send_half(dd, 1, first_block(dd))
        if dd in (2, 5):
            pl.semaphore_wait(up_sem, 1)
            for r in range(2):
                a_send_half(dd, r, 1)

    each(range(RING), a_rest)

    load(coli_in, coli)
    load(rowi_in.at[d], rowi)
    load(mom_in, mom)

    def b_copies(dd, src, dst, send, recv):
        b, row, rows = OWNS[dd]
        count = 0
        for m in MEMBERS[b]:
            slot = blocks_of(m).index(b)
            for xr in (1, 0):
                if (m, xr) != (dd, 0):
                    count += 1
                    pltpu.make_async_remote_copy(
                        src(xr),
                        dst(xr, slice(slot * BAND + row, slot * BAND + row + rows)),
                        send,
                        recv.at[slot],
                        device_id=at(y, xr, m),
                        device_id_type=MESH,
                    ).start()
        return count

    def own_rows(dd):
        b, row, rows = OWNS[dd]
        start = blocks_of(dd).index(b) * BAND + row
        return slice(start, start + rows)

    def band_part(xr, at_rows):
        return band.at[1 - xr, at_rows]

    def total_part(xr, at_rows):
        return total.at[at_rows, half_cols()]

    def gather_a(dd):
        b, row, rows = OWNS[dd]
        wait_rows(None, a_recv, rows, 2 * len(MEMBERS[b]) - 1)
        mine, other = part[1, own_rows(dd)], None
        for n, m in enumerate(MEMBERS[b]):
            if m != dd:
                mine = mine + from_a[2 * n, :rows]
            got = from_a[2 * n + 1, :rows]
            other = got if other is None else other + got
        from_y[y, :rows] = mine + other
        sums[0, :rows] = mine
        sums[1, :rows] = other
        pl.semaphore_wait(ring_sem, 2)
        for k in (4, 3, 5, 2, 6, 1, 7):
            pltpu.make_async_remote_copy(
                from_y.at[y, :rows], from_y.at[y, :rows], y_send, y_recv, device_id=at(ring(k), 0, dd), device_id_type=MESH
            ).start()
        b_copies(dd, lambda xr: sums.at[xr, :rows], band_part, b_send, b_recv)
        band[1, own_rows(dd)] = mine

    each(OWNS, gather_a)

    def b_wait(recv):
        def go(dd):
            for slot, b in enumerate(blocks_of(dd)):
                wait_rows(None, recv.at[slot], 2 * BAND - (OWNS[dd][2] if dd in owners_of(b) else 0))

        each(range(RING), go)

    for c in loads[8:]:
        c.wait()
    b_wait(b_recv)
    sent = invert(jnp.concatenate([band[0], band[1]], axis=1), rowi[...], coli[...])
    for c in range(2 * chunks):
        r, at_c = c // chunks, slice(512 * (c % chunks), 512 * (c % chunks + 1))
        res[r, :, at_c] = res[r, :, at_c] - sent[ROWS_DEV * c : ROWS_DEV * (c + 1)]

    def gather_y(dd):
        b, row, rows = OWNS[dd]
        wait_rows(None, y_recv, rows, ny - 1)
        whole = from_y[0, :rows]
        for n in range(1, ny):
            whole = whole + from_y[n, :rows]
        whole = whole * (1.0 / (2 * ny))
        sums[2, :rows] = whole
        b_copies(dd, lambda xr: sums.at[2, :rows], total_part, t_send, t_recv)
        total[own_rows(dd), half_cols()] = whole
        wait_rows(y_send, None, rows, ny - 1)
        for sem in (b_send, t_send):
            wait_rows(sem, None, rows, 2 * len(MEMBERS[b]) - 1)

    each(OWNS, gather_y)

    def a_sent(dd):
        rows = 2 * BAND - (OWNS[dd][2] if dd in OWNS else 0)
        wait_rows(a_send, None, rows)
        if dd in (2, 5):
            wait_rows(a_send, None, 2 * BAND)

    each(range(RING), a_sent)
    b_wait(t_recv)


def finish(
    cols,
    total, res, outer, mom, coli, rowi,
    outer_out, mom_out, res_out,
    outer_v, mom_v, out_sem,
):
    xl = lax.rem(lax.axis_index("island"), 2)
    wide = cols // 2
    writes = []

    def write(src, dst):
        writes.append(pltpu.make_async_copy(src, dst, out_sem.at[len(writes)]))
        writes[-1].start()

    def columns(r, n, width):
        return pl.ds(pl.multiple_of(lax.rem(xl + 1 + r, 2) * wide + n, 128), width)

    for r in range(2):
        write(res.at[r], res_out.at[0, :, columns(r, 0, wide)])
    hi, lo = split(total[...])
    half = dot(rowi[...], jnp.concatenate([hi, lo, hi], axis=0))
    step = 1024
    for c in range(cols // step):
        at_c = slice(step * c, step * (c + 1))
        tall = jnp.concatenate([half[:, 128 * q : 128 * (q + 1)] for q in range(c * step // 512, (c + 1) * step // 512)], axis=0)
        hi, lo = split(tall)
        update = dot(jnp.concatenate([hi, lo, hi], axis=1), coli[...])
        for q in range(step // 512):
            n = (c * step + 512 * q) % wide
            r = (c * step + 512 * q) // wide
            at_q = slice(step * c + 512 * q, step * c + 512 * (q + 1))
            u = update[ROWS_DEV * q : ROWS_DEV * (q + 1)]
            rel = jnp.where(r == xl, 1, 0)
            m = KEEP * mom[:, at_q] + u
            mom_v[:, at_q] = m
            outer_v[:, at_q] = outer[rel, :, n : n + 512] - OUTER_RATE * (u + KEEP * m)
        write(mom_v.at[:, at_c], mom_out.at[:, at_c])
        write(outer_v.at[:, at_c], outer_out.at[:, at_c])
    for c in writes:
        c.wait()


def solution(mesh):
    ny = mesh.shape["island"] // 2
    col_fwd, col_inv, row_fwd, row_inv = tables()

    def per_device(inner, outer, momentum, residual):
        rows, cols = outer.shape
        hc = cols * BAND // GROUP // 2
        f32, bf16 = jnp.float32, jnp.bfloat16
        dma, regular = pltpu.SemaphoreType.DMA, pltpu.SemaphoreType.REGULAR
        any_space = pl.BlockSpec(memory_space=pl.ANY)
        vmem = pl.BlockSpec(memory_space=pltpu.VMEM)
        in_hbm = lambda a: pltpu.with_memory_space_constraint(a, pltpu.HBM)
        tables_hbm = [jnp.asarray(a) for a in (col_fwd, col_inv, row_fwd, row_inv)]
        passed = pl.pallas_call(
            functools.partial(kernel, ny, cols),
            name="exchange",
            out_shape=[
                pltpu.VMEM((2 * BAND, 2 * hc), f32),
                pltpu.VMEM((2, rows, cols // 2), f32),
                pltpu.VMEM((2, rows, cols // 2), f32),
                pltpu.VMEM((rows, cols), f32),
                pltpu.VMEM(col_inv.shape, bf16),
                pltpu.VMEM(row_inv.shape[1:], bf16),
            ],
            in_specs=[any_space] * 8,
            out_specs=[vmem] * 6,
            scratch_shapes=[
                pltpu.VMEM((2, rows, cols // 2), bf16),
                pltpu.VMEM(col_fwd.shape, bf16),
                pltpu.VMEM(row_fwd.shape[1:], bf16),
                pltpu.VMEM((2, 2 * BAND, hc), f32),
                pltpu.VMEM((8, MOST, hc), f32),
                pltpu.VMEM((3, MOST, hc), f32),
                pltpu.VMEM((ny, MOST, hc), f32),
                pltpu.VMEM((2, 2 * BAND, hc), f32),
                dma((11,)), regular, regular,
                dma, dma, dma, dma, dma, dma((2,)), dma, dma((2,)),
            ],
            compiler_params=pltpu.CompilerParams(
                collective_id=0, has_side_effects=True, vmem_limit_bytes=24 * 1024 * 1024
            ),
        )(*map(in_hbm, (inner, outer, momentum, residual, *tables_hbm)))
        return tuple(
            pl.pallas_call(
                functools.partial(finish, cols),
                name="finish",
                out_shape=[
                    jax.ShapeDtypeStruct((rows, cols), f32),
                    jax.ShapeDtypeStruct((rows, cols), f32),
                    jax.ShapeDtypeStruct((1, rows, cols), f32),
                ],
                in_specs=[vmem] * 6,
                out_specs=[any_space] * 3,
                scratch_shapes=[pltpu.VMEM((rows, cols), f32), pltpu.VMEM((rows, cols), f32), dma((8,))],
                compiler_params=pltpu.CompilerParams(vmem_limit_bytes=24 * 1024 * 1024),
            )(*passed)
        )

    return jax.shard_map(
        per_device,
        mesh=mesh,
        in_specs=(P("island", "fsdp", None), P("fsdp", None), P("fsdp", None), P("island", "fsdp", None)),
        out_specs=(P("fsdp", None), P("fsdp", None), P("island", "fsdp", None)),
        check_vma=False,
    )
```

```python
import functools

import jax
import jax.numpy as jnp
import ml_dtypes
import numpy as np
from jax import lax
from jax.experimental import pallas as pl
from jax.experimental.pallas import tpu as pltpu
from jax.sharding import PartitionSpec as P

GROUP = 128
BAND = 32
ROWS_DEV = 48
RING = 8
OUTER_RATE = 0.7
KEEP = 0.9
MESH = pl.DeviceIdType.MESH
BF16 = ml_dtypes.bfloat16


def split_np(a):
    hi = a.astype(np.float32).astype(BF16)
    lo = (a - hi.astype(np.float64)).astype(np.float32).astype(BF16)
    return hi, lo


def cosine_low():
    freq = np.arange(BAND, dtype=np.float64)[:, None]
    place = np.arange(GROUP, dtype=np.float64)[None, :]
    table = np.cos(np.pi * (2.0 * place + 1.0) * freq / (2.0 * GROUP))
    scale = np.where(freq == 0, np.sqrt(1.0 / GROUP), np.sqrt(2.0 / GROUP))
    return table * scale


def tables():
    low = cosine_low()
    diag = np.zeros((4 * GROUP, 4 * BAND))
    for q in range(4):
        diag[q * GROUP : (q + 1) * GROUP, q * BAND : (q + 1) * BAND] = low.T
    hi, lo = split_np(diag)
    col_fwd = np.concatenate([hi, lo], axis=1)
    hi, lo = split_np(diag.T)
    col_inv = np.concatenate([hi, hi, lo], axis=0)
    row_fwd = np.zeros((RING, 2 * BAND, 3 * ROWS_DEV), BF16)
    row_inv = np.zeros((RING, ROWS_DEV, 3 * 2 * BAND), BF16)
    for d in range(RING):
        rows = d * ROWS_DEV + np.arange(ROWS_DEV)
        first, last = rows[0] // GROUP, rows[-1] // GROUP
        part = np.zeros((2 * BAND, ROWS_DEV))
        for slot, b in enumerate((first, last)):
            if slot == 1 and first == last:
                continue
            inside = rows // GROUP == b
            part[slot * BAND : (slot + 1) * BAND, inside] = low[:, rows[inside] % GROUP]
        hi, lo = split_np(part)
        row_fwd[d] = np.concatenate([hi, hi, lo], axis=1)
        hi, lo = split_np(part.T)
        row_inv[d] = np.concatenate([hi, hi, lo], axis=1)
    return col_fwd, col_inv, row_fwd, row_inv


def split(a):
    hi = a.astype(jnp.bfloat16)
    lo = (a - hi.astype(jnp.float32)).astype(jnp.bfloat16)
    return hi, lo


def dot(a, b):
    return jnp.dot(a, b, preferred_element_type=jnp.float32)


def invert(coef, rowi, coli):
    hi, lo = split(coef)
    wide = dot(rowi, jnp.concatenate([hi, lo, hi], axis=0))
    tall = jnp.concatenate([wide[:, 128 * c : 128 * (c + 1)] for c in range(wide.shape[1] // 128)], axis=0)
    hi, lo = split(tall)
    return dot(jnp.concatenate([hi, lo, hi], axis=1), coli)


OWNS = (
    [], [(0, 0, 24)], [(0, 24, 8), (1, 0, 8)], [(1, 8, 8)], [(1, 16, 8)], [(1, 24, 8), (2, 0, 8)], [(2, 8, 24)], [],
)
MEMBERS = ((0, 1, 2), (2, 3, 4, 5), (5, 6, 7))
MOST = 24


def blocks_of(d):
    return [b for b in range(3) if d in MEMBERS[b]]


def share(d, b):
    found = [n for n, own in enumerate(OWNS[d]) if own[0] == b]
    return (found[0], *OWNS[d][found[0]][1:]) if found else (None, 0, 0)


def owned(d):
    return [own[0] for own in OWNS[d]]


def greets(d, b, m):
    return b in owned(d) and not (b == 1 and m in (2, 5))


def greetings(d):
    return sum(greets(m, b, d) for b in blocks_of(d) for m, _ in partners(d, b, (1, 0))) + (4 if OWNS[d] else 0)


def partners(d, b, halves):
    found = [(m, xr) for m in MEMBERS[b] for xr in halves if (m, xr) != (d, 0)]
    return sorted(found, key=lambda p: (-abs(p[0] // 2 - d // 2) - p[1], p[0] == d, p))


def kernel(
    ny, cols,
    inner_in, outer_in, mom_in, res_in, colf_in, coli_in, rowf_in, rowi_in,
    total, res, outer, mom, coli, rowi,
    inner, colf, rowf, part, from_a, sums, from_y, band,
    load_sem, up_sem, ring_sem,
    a_send, a_recv, y_send, y_recv, b_send, b_recv, t_send, t_recv,
):
    hc = cols * BAND // GROUP // 2
    wide = cols // 2
    i, f = lax.axis_index("island"), lax.axis_index("fsdp")
    y, xl = lax.div(i, 2), lax.rem(i, 2)
    d = lax.rem(f, RING)
    base = f - d

    def at(yy, xr, dd):
        return (yy * 2 + (1 - xl if xr else xl), base + dd)

    def ring(k):
        return lax.rem(y + k, ny)

    def signal(sem, where):
        pl.semaphore_signal(sem, 1, device_id=where, device_id_type=MESH)

    def each(devices, body):
        for dd in devices:
            pl.when(d == dd)(functools.partial(body, dd))

    def wide_cols(r):
        return pl.ds(pl.multiple_of((xl if r else 1 - xl) * wide, 128), wide)

    loads = []

    def load(src, dst):
        loads.append(pltpu.make_async_copy(src, dst, load_sem.at[len(loads)]))
        loads[-1].start()

    load(inner_in.at[0, :, wide_cols(0)], inner.at[0])
    load(res_in.at[0, :, wide_cols(0)], res.at[0])
    load(outer_in.at[:, wide_cols(0)], outer.at[0])
    load(colf_in, colf)

    bar = pltpu.get_barrier_semaphore()

    def greet(dd):
        for b in blocks_of(dd):
            for m, xr in partners(dd, b, (1, 0)):
                if greets(dd, b, m):
                    signal(bar, at(y, xr, m))

        for k in (2, ny - 2, 1, ny - 1) if OWNS[dd] else ():
            signal(bar, at(ring(k), 0, dd))

    each(range(RING), greet)

    load(inner_in.at[0, :, wide_cols(1)], inner.at[1])
    load(res_in.at[0, :, wide_cols(1)], res.at[1])
    load(outer_in.at[:, wide_cols(1)], outer.at[1])
    load(rowf_in.at[d], rowf)

    @pl.when((d != 2) & (d != 5))
    def _():
        band[:, BAND:] = jnp.zeros((2, BAND, hc), jnp.float32)
        total[BAND:] = jnp.zeros((BAND, 2 * hc), jnp.float32)

    chunks = wide // 512

    def forward(r):
        acc = outer[r] - inner[r].astype(jnp.float32) + res[r]
        res[r] = acc
        hi, lo = split(jnp.concatenate([acc[:, 512 * c : 512 * (c + 1)] for c in range(chunks)], axis=0))
        prod = dot(hi, colf[...])
        tall = prod[:, :128] + prod[:, 128:] + dot(lo, colf[:, :128])
        hi, lo = split(jnp.concatenate([tall[ROWS_DEV * c : ROWS_DEV * (c + 1)] for c in range(chunks)], axis=1))
        part[r] = dot(rowf[...], jnp.concatenate([hi, lo, hi], axis=0))

    def half_cols():
        return pl.ds(pl.multiple_of(xl * hc, 128), hc)

    def wait_rows(send, recv, rows, count=1):
        ref = part.at[0, :rows] if count == 1 else from_a.at[0, :count, :rows]
        sems = (send, send) if recv is None else (recv, recv)
        copy = pltpu.make_async_remote_copy(ref, ref, *sems, device_id=at(y, 1, d), device_id_type=MESH)
        copy.wait_recv() if recv is not None else copy.wait_send()

    def a_send_half(dd, r, b):
        slot = blocks_of(dd).index(b)
        for to, xr in partners(dd, b, (1 - r,)):
            own, row, rows = share(to, b)
            if not rows:
                continue
            pltpu.make_async_remote_copy(
                part.at[r, slot * BAND + row : slot * BAND + row + rows],
                from_a.at[own, MEMBERS[b].index(dd) * 2 + xr, :rows],
                a_send,
                a_recv.at[own],
                device_id=at(y, xr, to),
                device_id_type=MESH,
            ).start()

    def first_block(dd):
        return 2 if dd == 5 else blocks_of(dd)[0]

    for c in loads[:4]:
        c.wait()
    loads[7].wait()
    forward(0)
    expected = greetings(0)
    for dd in range(1, RING):
        expected = jnp.where(d == dd, greetings(dd), expected)
    pl.semaphore_wait(bar, expected)

    @pl.when((d == 3) | (d == 4))
    def _():
        signal(up_sem, at(y, 0, jnp.where(d == 3, 2, 5)))

    def a_start(dd):
        a_send_half(dd, 0, first_block(dd))
        for k in (2, ny - 2) if OWNS[dd] else ():
            signal(ring_sem, at(ring(k), 0, dd))

    each(range(RING), a_start)

    for c in loads[4:7]:
        c.wait()
    forward(1)

    def a_rest(dd):
        a_send_half(dd, 1, first_block(dd))
        if dd in (2, 5):
            pl.semaphore_wait(up_sem, 1)
            for r in range(2):
                a_send_half(dd, r, 1)

    each(range(RING), a_rest)

    load(coli_in, coli)
    load(rowi_in.at[d], rowi)
    load(mom_in, mom)

    def b_copies(dd, b, src, dst, send, recv):
        own, row, rows = share(dd, b)
        for m, xr in partners(dd, b, (1, 0)):
            slot = blocks_of(m).index(b)
            pltpu.make_async_remote_copy(
                src(own, xr, rows),
                dst(xr, slice(slot * BAND + row, slot * BAND + row + rows)),
                send,
                recv.at[slot],
                device_id=at(y, xr, m),
                device_id_type=MESH,
            ).start()

    def own_rows(dd, b):
        start = blocks_of(dd).index(b) * BAND + share(dd, b)[1]
        return slice(start, start + share(dd, b)[2])

    def band_part(xr, at_rows):
        return band.at[1 - xr, at_rows]

    def total_part(xr, at_rows):
        return total.at[at_rows, half_cols()]

    def gather_a(dd):
        for n, (b, row, rows) in enumerate(OWNS[dd]):
            wait_rows(None, a_recv.at[n], rows, 2 * len(MEMBERS[b]) - 1)
            mine, other = part[1, own_rows(dd, b)], None
            for k, m in enumerate(MEMBERS[b]):
                if m != dd:
                    mine = mine + from_a[n, 2 * k, :rows]
                got = from_a[n, 2 * k + 1, :rows]
                other = got if other is None else other + got
            from_y[n, y, :rows] = mine + other
            sums[n, 0, :rows] = mine
            sums[n, 1, :rows] = other
            if n == 0:
                pl.semaphore_wait(ring_sem, 2)
            for k in (4, 3, 5, 2, 6, 1, 7):
                pltpu.make_async_remote_copy(
                    from_y.at[n, y, :rows], from_y.at[n, y, :rows], y_send.at[n], y_recv.at[n],
                    device_id=at(ring(k), 0, dd), device_id_type=MESH,
                ).start()
            b_copies(dd, b, lambda own, xr, rows: sums.at[own, xr, :rows], band_part, b_send, b_recv)
            band[1, own_rows(dd, b)] = mine

    each(range(RING), gather_a)

    def b_wait(recv):
        def go(dd):
            for slot, b in enumerate(blocks_of(dd)):
                wait_rows(None, recv.at[slot], 2 * BAND - share(dd, b)[2])

        each(range(RING), go)

    for c in loads[8:]:
        c.wait()
    b_wait(b_recv)
    sent = invert(jnp.concatenate([band[0], band[1]], axis=1), rowi[...], coli[...])
    for c in range(2 * chunks):
        r, at_c = c // chunks, slice(512 * (c % chunks), 512 * (c % chunks + 1))
        res[r, :, at_c] = res[r, :, at_c] - sent[ROWS_DEV * c : ROWS_DEV * (c + 1)]

    def gather_y(dd):
        for n, (b, row, rows) in enumerate(OWNS[dd]):
            wait_rows(None, y_recv.at[n], rows, ny - 1)
            whole = from_y[n, 0, :rows]
            for k in range(1, ny):
                whole = whole + from_y[n, k, :rows]
            whole = whole * (1.0 / (2 * ny))
            sums[n, 2, :rows] = whole
            b_copies(dd, b, lambda own, xr, rows: sums.at[own, 2, :rows], total_part, t_send, t_recv)
            total[own_rows(dd, b), half_cols()] = whole
        for b in blocks_of(dd):
            wait_rows(a_send, None, 2 * BAND - share(dd, b)[2])
        for n, (b, row, rows) in enumerate(OWNS[dd]):
            wait_rows(y_send.at[n], None, rows, ny - 1)
            for sem in (b_send, t_send):
                wait_rows(sem, None, rows, 2 * len(MEMBERS[b]) - 1)

    each(range(RING), gather_y)
    b_wait(t_recv)


def finish(
    cols,
    total, res, outer, mom, coli, rowi,
    outer_out, mom_out, res_out,
    outer_v, mom_v, out_sem,
):
    xl = lax.rem(lax.axis_index("island"), 2)
    wide = cols // 2
    writes = []

    def write(src, dst):
        writes.append(pltpu.make_async_copy(src, dst, out_sem.at[len(writes)]))
        writes[-1].start()

    def columns(r, n, width):
        return pl.ds(pl.multiple_of(lax.rem(xl + 1 + r, 2) * wide + n, 128), width)

    for r in range(2):
        write(res.at[r], res_out.at[0, :, columns(r, 0, wide)])
    hi, lo = split(total[...])
    half = dot(rowi[...], jnp.concatenate([hi, lo, hi], axis=0))
    step = 1024
    for c in range(cols // step):
        at_c = slice(step * c, step * (c + 1))
        tall = jnp.concatenate([half[:, 128 * q : 128 * (q + 1)] for q in range(c * step // 512, (c + 1) * step // 512)], axis=0)
        hi, lo = split(tall)
        update = dot(jnp.concatenate([hi, lo, hi], axis=1), coli[...])
        for q in range(step // 512):
            n = (c * step + 512 * q) % wide
            r = (c * step + 512 * q) // wide
            at_q = slice(step * c + 512 * q, step * c + 512 * (q + 1))
            u = update[ROWS_DEV * q : ROWS_DEV * (q + 1)]
            rel = jnp.where(r == xl, 1, 0)
            m = KEEP * mom[:, at_q] + u
            mom_v[:, at_q] = m
            outer_v[:, at_q] = outer[rel, :, n : n + 512] - OUTER_RATE * (u + KEEP * m)
        write(mom_v.at[:, at_c], mom_out.at[:, at_c])
        write(outer_v.at[:, at_c], outer_out.at[:, at_c])
    for c in writes:
        c.wait()


def solution(mesh):
    ny = mesh.shape["island"] // 2
    col_fwd, col_inv, row_fwd, row_inv = tables()

    def per_device(inner, outer, momentum, residual):
        rows, cols = outer.shape
        hc = cols * BAND // GROUP // 2
        f32, bf16 = jnp.float32, jnp.bfloat16
        dma, regular = pltpu.SemaphoreType.DMA, pltpu.SemaphoreType.REGULAR
        any_space = pl.BlockSpec(memory_space=pl.ANY)
        vmem = pl.BlockSpec(memory_space=pltpu.VMEM)
        in_hbm = lambda a: pltpu.with_memory_space_constraint(a, pltpu.HBM)
        tables_hbm = [jnp.asarray(a) for a in (col_fwd, col_inv, row_fwd, row_inv)]
        passed = pl.pallas_call(
            functools.partial(kernel, ny, cols),
            name="exchange",
            out_shape=[
                pltpu.VMEM((2 * BAND, 2 * hc), f32),
                pltpu.VMEM((2, rows, cols // 2), f32),
                pltpu.VMEM((2, rows, cols // 2), f32),
                pltpu.VMEM((rows, cols), f32),
                pltpu.VMEM(col_inv.shape, bf16),
                pltpu.VMEM(row_inv.shape[1:], bf16),
            ],
            in_specs=[any_space] * 8,
            out_specs=[vmem] * 6,
            scratch_shapes=[
                pltpu.VMEM((2, rows, cols // 2), bf16),
                pltpu.VMEM(col_fwd.shape, bf16),
                pltpu.VMEM(row_fwd.shape[1:], bf16),
                pltpu.VMEM((2, 2 * BAND, hc), f32),
                pltpu.VMEM((2, 8, MOST, hc), f32),
                pltpu.VMEM((2, 3, MOST, hc), f32),
                pltpu.VMEM((2, ny, MOST, hc), f32),
                pltpu.VMEM((2, 2 * BAND, hc), f32),
                dma((11,)), regular, regular,
                dma, dma((2,)), dma((2,)), dma((2,)), dma, dma((2,)), dma, dma((2,)),
            ],
            compiler_params=pltpu.CompilerParams(
                collective_id=0, has_side_effects=True, vmem_limit_bytes=24 * 1024 * 1024
            ),
        )(*map(in_hbm, (inner, outer, momentum, residual, *tables_hbm)))
        return tuple(
            pl.pallas_call(
                functools.partial(finish, cols),
                name="finish",
                out_shape=[
                    jax.ShapeDtypeStruct((rows, cols), f32),
                    jax.ShapeDtypeStruct((rows, cols), f32),
                    jax.ShapeDtypeStruct((1, rows, cols), f32),
                ],
                in_specs=[vmem] * 6,
                out_specs=[any_space] * 3,
                scratch_shapes=[pltpu.VMEM((rows, cols), f32), pltpu.VMEM((rows, cols), f32), dma((8,))],
                compiler_params=pltpu.CompilerParams(vmem_limit_bytes=24 * 1024 * 1024),
            )(*passed)
        )

    return jax.shard_map(
        per_device,
        mesh=mesh,
        in_specs=(P("island", "fsdp", None), P("fsdp", None), P("fsdp", None), P("island", "fsdp", None)),
        out_specs=(P("fsdp", None), P("fsdp", None), P("island", "fsdp", None)),
        check_vma=False,
    )
```

```python
import functools

import jax
import jax.numpy as jnp
import ml_dtypes
import numpy as np
from jax import lax
from jax.experimental import pallas as pl
from jax.experimental.pallas import tpu as pltpu
from jax.sharding import PartitionSpec as P

GROUP = 128
BAND = 32
ROWS_DEV = 48
RING = 8
OUTER_RATE = 0.7
KEEP = 0.9
MESH = pl.DeviceIdType.MESH
BF16 = ml_dtypes.bfloat16


def split_np(a):
    hi = a.astype(np.float32).astype(BF16)
    lo = (a - hi.astype(np.float64)).astype(np.float32).astype(BF16)
    return hi, lo


def cosine_low():
    freq = np.arange(BAND, dtype=np.float64)[:, None]
    place = np.arange(GROUP, dtype=np.float64)[None, :]
    table = np.cos(np.pi * (2.0 * place + 1.0) * freq / (2.0 * GROUP))
    scale = np.where(freq == 0, np.sqrt(1.0 / GROUP), np.sqrt(2.0 / GROUP))
    return table * scale


def tables():
    low = cosine_low()
    diag = np.zeros((4 * GROUP, 4 * BAND))
    for q in range(4):
        diag[q * GROUP : (q + 1) * GROUP, q * BAND : (q + 1) * BAND] = low.T
    hi, lo = split_np(diag)
    col_fwd = np.concatenate([hi, lo], axis=1)
    hi, lo = split_np(diag.T)
    col_inv = np.concatenate([hi, hi, lo], axis=0)
    row_fwd = np.zeros((RING, 2 * BAND, 3 * ROWS_DEV), BF16)
    row_inv = np.zeros((RING, ROWS_DEV, 3 * 2 * BAND), BF16)
    for d in range(RING):
        rows = d * ROWS_DEV + np.arange(ROWS_DEV)
        first, last = rows[0] // GROUP, rows[-1] // GROUP
        part = np.zeros((2 * BAND, ROWS_DEV))
        for slot, b in enumerate((first, last)):
            if slot == 1 and first == last:
                continue
            inside = rows // GROUP == b
            part[slot * BAND : (slot + 1) * BAND, inside] = low[:, rows[inside] % GROUP]
        hi, lo = split_np(part)
        row_fwd[d] = np.concatenate([hi, hi, lo], axis=1)
        hi, lo = split_np(part.T)
        row_inv[d] = np.concatenate([hi, hi, lo], axis=1)
    return col_fwd, col_inv, row_fwd, row_inv


def split(a):
    hi = a.astype(jnp.bfloat16)
    lo = (a - hi.astype(jnp.float32)).astype(jnp.bfloat16)
    return hi, lo


def dot(a, b):
    return jnp.dot(a, b, preferred_element_type=jnp.float32)


def invert(coef, rowi, coli):
    hi, lo = split(coef)
    wide = dot(rowi, jnp.concatenate([hi, lo, hi], axis=0))
    tall = jnp.concatenate([wide[:, 128 * c : 128 * (c + 1)] for c in range(wide.shape[1] // 128)], axis=0)
    hi, lo = split(tall)
    return dot(jnp.concatenate([hi, lo, hi], axis=1), coli)


OWNS = (
    [], [(0, 0, 24)], [(0, 24, 8), (1, 0, 8)], [(1, 8, 8)], [(1, 16, 8)], [(1, 24, 8), (2, 0, 8)], [(2, 8, 16)], [(2, 24, 8)],
)
MEMBERS = ((0, 1, 2), (2, 3, 4, 5), (5, 6, 7))
MOST = 24


def blocks_of(d):
    return [b for b in range(3) if d in MEMBERS[b]]


def share(d, b):
    found = [n for n, own in enumerate(OWNS[d]) if own[0] == b]
    return (found[0], *OWNS[d][found[0]][1:]) if found else (None, 0, 0)


def owned(d):
    return [own[0] for own in OWNS[d]]


def greets(d, b, m):
    return b in owned(d) and not (b == 1 and m in (2, 5))


def greetings(d):
    return sum(greets(m, b, d) for b in blocks_of(d) for m, _ in partners(d, b, (1, 0))) + (4 if OWNS[d] else 0)


def partners(d, b, halves):
    found = [(m, xr) for m in MEMBERS[b] for xr in halves if (m, xr) != (d, 0)]
    return sorted(found, key=lambda p: (-abs(p[0] // 2 - d // 2) - p[1], p[0] == d, p))


def kernel(
    ny, cols,
    inner_in, outer_in, mom_in, res_in, colf_in, coli_in, rowf_in, rowi_in,
    total, res, outer, mom, coli, rowi,
    inner, colf, rowf, part, from_a, sums, from_y, band,
    load_sem, up_sem, ring_sem,
    a_send, a_recv, y_send, y_recv, b_send, b_recv, t_send, t_recv,
):
    hc = cols * BAND // GROUP // 2
    wide = cols // 2
    i, f = lax.axis_index("island"), lax.axis_index("fsdp")
    y, xl = lax.div(i, 2), lax.rem(i, 2)
    d = lax.rem(f, RING)
    base = f - d

    def at(yy, xr, dd):
        return (yy * 2 + (1 - xl if xr else xl), base + dd)

    def ring(k):
        return lax.rem(y + k, ny)

    def signal(sem, where):
        pl.semaphore_signal(sem, 1, device_id=where, device_id_type=MESH)

    def each(devices, body):
        for dd in devices:
            pl.when(d == dd)(functools.partial(body, dd))

    def wide_cols(r):
        return pl.ds(pl.multiple_of((xl if r else 1 - xl) * wide, 128), wide)

    loads = []

    def load(src, dst):
        loads.append(pltpu.make_async_copy(src, dst, load_sem.at[len(loads)]))
        loads[-1].start()

    load(inner_in.at[0, :, wide_cols(0)], inner.at[0])
    load(res_in.at[0, :, wide_cols(0)], res.at[0])
    load(outer_in.at[:, wide_cols(0)], outer.at[0])
    load(colf_in, colf)

    bar = pltpu.get_barrier_semaphore()

    def greet(dd):
        for b in blocks_of(dd):
            for m, xr in partners(dd, b, (1, 0)):
                if greets(dd, b, m):
                    signal(bar, at(y, xr, m))

        for k in (2, ny - 2, 1, ny - 1) if OWNS[dd] else ():
            signal(bar, at(ring(k), 0, dd))

    each(range(RING), greet)

    load(inner_in.at[0, :, wide_cols(1)], inner.at[1])
    load(res_in.at[0, :, wide_cols(1)], res.at[1])
    load(outer_in.at[:, wide_cols(1)], outer.at[1])
    load(rowf_in.at[d], rowf)

    @pl.when((d != 2) & (d != 5))
    def _():
        band[:, BAND:] = jnp.zeros((2, BAND, hc), jnp.float32)
        total[BAND:] = jnp.zeros((BAND, 2 * hc), jnp.float32)

    chunks = wide // 512

    def forward(r):
        acc = outer[r] - inner[r].astype(jnp.float32) + res[r]
        res[r] = acc
        hi, lo = split(jnp.concatenate([acc[:, 512 * c : 512 * (c + 1)] for c in range(chunks)], axis=0))
        prod = dot(hi, colf[...])
        tall = prod[:, :128] + prod[:, 128:] + dot(lo, colf[:, :128])
        hi, lo = split(jnp.concatenate([tall[ROWS_DEV * c : ROWS_DEV * (c + 1)] for c in range(chunks)], axis=1))
        part[r] = dot(rowf[...], jnp.concatenate([hi, lo, hi], axis=0))

    def half_cols():
        return pl.ds(pl.multiple_of(xl * hc, 128), hc)

    def wait_rows(send, recv, rows, count=1):
        ref = part.at[0, :rows] if count == 1 else from_a.at[0, :count, :rows]
        sems = (send, send) if recv is None else (recv, recv)
        copy = pltpu.make_async_remote_copy(ref, ref, *sems, device_id=at(y, 1, d), device_id_type=MESH)
        copy.wait_recv() if recv is not None else copy.wait_send()

    def a_send_half(dd, r, b):
        slot = blocks_of(dd).index(b)
        for to, xr in partners(dd, b, (1 - r,)):
            own, row, rows = share(to, b)
            if not rows:
                continue
            pltpu.make_async_remote_copy(
                part.at[r, slot * BAND + row : slot * BAND + row + rows],
                from_a.at[own, MEMBERS[b].index(dd) * 2 + xr, :rows],
                a_send,
                a_recv.at[own],
                device_id=at(y, xr, to),
                device_id_type=MESH,
            ).start()

    def first_block(dd):
        return 2 if dd == 5 else blocks_of(dd)[0]

    for c in loads[:4]:
        c.wait()
    loads[7].wait()
    forward(0)
    expected = greetings(0)
    for dd in range(1, RING):
        expected = jnp.where(d == dd, greetings(dd), expected)
    pl.semaphore_wait(bar, expected)

    @pl.when((d == 3) | (d == 4))
    def _():
        signal(up_sem, at(y, 0, jnp.where(d == 3, 2, 5)))

    def a_start(dd):
        a_send_half(dd, 0, first_block(dd))
        for k in (2, ny - 2) if OWNS[dd] else ():
            signal(ring_sem, at(ring(k), 0, dd))

    each(range(RING), a_start)

    for c in loads[4:7]:
        c.wait()
    forward(1)

    def a_rest(dd):
        a_send_half(dd, 1, first_block(dd))
        if dd in (2, 5):
            pl.semaphore_wait(up_sem, 1)
            for r in range(2):
                a_send_half(dd, r, 1)

    each(range(RING), a_rest)

    load(coli_in, coli)
    load(rowi_in.at[d], rowi)
    load(mom_in, mom)

    def b_copies(dd, b, src, dst, send, recv):
        own, row, rows = share(dd, b)
        for m, xr in partners(dd, b, (1, 0)):
            slot = blocks_of(m).index(b)
            pltpu.make_async_remote_copy(
                src(own, xr, rows),
                dst(xr, slice(slot * BAND + row, slot * BAND + row + rows)),
                send,
                recv.at[slot],
                device_id=at(y, xr, m),
                device_id_type=MESH,
            ).start()

    def own_rows(dd, b):
        start = blocks_of(dd).index(b) * BAND + share(dd, b)[1]
        return slice(start, start + share(dd, b)[2])

    def band_part(xr, at_rows):
        return band.at[1 - xr, at_rows]

    def total_part(xr, at_rows):
        return total.at[at_rows, half_cols()]

    def gather_a(dd):
        for n, (b, row, rows) in enumerate(OWNS[dd]):
            wait_rows(None, a_recv.at[n], rows, 2 * len(MEMBERS[b]) - 1)
            mine, other = part[1, own_rows(dd, b)], None
            for k, m in enumerate(MEMBERS[b]):
                if m != dd:
                    mine = mine + from_a[n, 2 * k, :rows]
                got = from_a[n, 2 * k + 1, :rows]
                other = got if other is None else other + got
            from_y[n, y, :rows] = mine + other
            sums[n, 0, :rows] = mine
            sums[n, 1, :rows] = other
            if n == 0:
                pl.semaphore_wait(ring_sem, 2)
            for k in (4, 3, 5, 2, 6, 1, 7):
                pltpu.make_async_remote_copy(
                    from_y.at[n, y, :rows], from_y.at[n, y, :rows], y_send.at[n], y_recv.at[n],
                    device_id=at(ring(k), 0, dd), device_id_type=MESH,
                ).start()
            b_copies(dd, b, lambda own, xr, rows: sums.at[own, xr, :rows], band_part, b_send, b_recv)
            band[1, own_rows(dd, b)] = mine

    each(range(RING), gather_a)

    def b_wait(recv):
        def go(dd):
            for slot, b in enumerate(blocks_of(dd)):
                wait_rows(None, recv.at[slot], 2 * BAND - share(dd, b)[2])

        each(range(RING), go)

    for c in loads[8:]:
        c.wait()
    b_wait(b_recv)
    sent = invert(jnp.concatenate([band[0], band[1]], axis=1), rowi[...], coli[...])
    for c in range(2 * chunks):
        r, at_c = c // chunks, slice(512 * (c % chunks), 512 * (c % chunks + 1))
        res[r, :, at_c] = res[r, :, at_c] - sent[ROWS_DEV * c : ROWS_DEV * (c + 1)]

    def gather_y(dd):
        for n, (b, row, rows) in enumerate(OWNS[dd]):
            wait_rows(None, y_recv.at[n], rows, ny - 1)
            whole = from_y[n, 0, :rows]
            for k in range(1, ny):
                whole = whole + from_y[n, k, :rows]
            whole = whole * (1.0 / (2 * ny))
            sums[n, 2, :rows] = whole
            b_copies(dd, b, lambda own, xr, rows: sums.at[own, 2, :rows], total_part, t_send, t_recv)
            total[own_rows(dd, b), half_cols()] = whole
        for b in blocks_of(dd):
            wait_rows(a_send, None, 2 * BAND - share(dd, b)[2])
        for n, (b, row, rows) in enumerate(OWNS[dd]):
            wait_rows(y_send.at[n], None, rows, ny - 1)
            for sem in (b_send, t_send):
                wait_rows(sem, None, rows, 2 * len(MEMBERS[b]) - 1)

    each(range(RING), gather_y)
    b_wait(t_recv)


def finish(
    cols,
    total, res, outer, mom, coli, rowi,
    outer_out, mom_out, res_out,
    outer_v, mom_v, out_sem,
):
    xl = lax.rem(lax.axis_index("island"), 2)
    wide = cols // 2
    writes = []

    def write(src, dst):
        writes.append(pltpu.make_async_copy(src, dst, out_sem.at[len(writes)]))
        writes[-1].start()

    def columns(r, n, width):
        return pl.ds(pl.multiple_of(lax.rem(xl + 1 + r, 2) * wide + n, 128), width)

    for r in range(2):
        write(res.at[r], res_out.at[0, :, columns(r, 0, wide)])
    hi, lo = split(total[...])
    half = dot(rowi[...], jnp.concatenate([hi, lo, hi], axis=0))
    step = 1024
    for c in range(cols // step):
        at_c = slice(step * c, step * (c + 1))
        tall = jnp.concatenate([half[:, 128 * q : 128 * (q + 1)] for q in range(c * step // 512, (c + 1) * step // 512)], axis=0)
        hi, lo = split(tall)
        update = dot(jnp.concatenate([hi, lo, hi], axis=1), coli[...])
        for q in range(step // 512):
            n = (c * step + 512 * q) % wide
            r = (c * step + 512 * q) // wide
            at_q = slice(step * c + 512 * q, step * c + 512 * (q + 1))
            u = update[ROWS_DEV * q : ROWS_DEV * (q + 1)]
            rel = jnp.where(r == xl, 1, 0)
            m = KEEP * mom[:, at_q] + u
            mom_v[:, at_q] = m
            outer_v[:, at_q] = outer[rel, :, n : n + 512] - OUTER_RATE * (u + KEEP * m)
        write(mom_v.at[:, at_c], mom_out.at[:, at_c])
        write(outer_v.at[:, at_c], outer_out.at[:, at_c])
    for c in writes:
        c.wait()


def solution(mesh):
    ny = mesh.shape["island"] // 2
    col_fwd, col_inv, row_fwd, row_inv = tables()

    def per_device(inner, outer, momentum, residual):
        rows, cols = outer.shape
        hc = cols * BAND // GROUP // 2
        f32, bf16 = jnp.float32, jnp.bfloat16
        dma, regular = pltpu.SemaphoreType.DMA, pltpu.SemaphoreType.REGULAR
        any_space = pl.BlockSpec(memory_space=pl.ANY)
        vmem = pl.BlockSpec(memory_space=pltpu.VMEM)
        in_hbm = lambda a: pltpu.with_memory_space_constraint(a, pltpu.HBM)
        tables_hbm = [jnp.asarray(a) for a in (col_fwd, col_inv, row_fwd, row_inv)]
        passed = pl.pallas_call(
            functools.partial(kernel, ny, cols),
            name="exchange",
            out_shape=[
                pltpu.VMEM((2 * BAND, 2 * hc), f32),
                pltpu.VMEM((2, rows, cols // 2), f32),
                pltpu.VMEM((2, rows, cols // 2), f32),
                pltpu.VMEM((rows, cols), f32),
                pltpu.VMEM(col_inv.shape, bf16),
                pltpu.VMEM(row_inv.shape[1:], bf16),
            ],
            in_specs=[any_space] * 8,
            out_specs=[vmem] * 6,
            scratch_shapes=[
                pltpu.VMEM((2, rows, cols // 2), bf16),
                pltpu.VMEM(col_fwd.shape, bf16),
                pltpu.VMEM(row_fwd.shape[1:], bf16),
                pltpu.VMEM((2, 2 * BAND, hc), f32),
                pltpu.VMEM((2, 8, MOST, hc), f32),
                pltpu.VMEM((2, 3, MOST, hc), f32),
                pltpu.VMEM((2, ny, MOST, hc), f32),
                pltpu.VMEM((2, 2 * BAND, hc), f32),
                dma((11,)), regular, regular,
                dma, dma((2,)), dma((2,)), dma((2,)), dma, dma((2,)), dma, dma((2,)),
            ],
            compiler_params=pltpu.CompilerParams(
                collective_id=0, has_side_effects=True, vmem_limit_bytes=24 * 1024 * 1024
            ),
        )(*map(in_hbm, (inner, outer, momentum, residual, *tables_hbm)))
        return tuple(
            pl.pallas_call(
                functools.partial(finish, cols),
                name="finish",
                out_shape=[
                    jax.ShapeDtypeStruct((rows, cols), f32),
                    jax.ShapeDtypeStruct((rows, cols), f32),
                    jax.ShapeDtypeStruct((1, rows, cols), f32),
                ],
                in_specs=[vmem] * 6,
                out_specs=[any_space] * 3,
                scratch_shapes=[pltpu.VMEM((rows, cols), f32), pltpu.VMEM((rows, cols), f32), dma((8,))],
                compiler_params=pltpu.CompilerParams(vmem_limit_bytes=24 * 1024 * 1024),
            )(*passed)
        )

    return jax.shard_map(
        per_device,
        mesh=mesh,
        in_specs=(P("island", "fsdp", None), P("fsdp", None), P("fsdp", None), P("island", "fsdp", None)),
        out_specs=(P("fsdp", None), P("fsdp", None), P("island", "fsdp", None)),
        check_vma=False,
    )
```

```python
import functools

import jax
import jax.numpy as jnp
import ml_dtypes
import numpy as np
from jax import lax
from jax.experimental import pallas as pl
from jax.experimental.pallas import tpu as pltpu
from jax.sharding import PartitionSpec as P

GROUP = 128
BAND = 32
ROWS_DEV = 48
RING = 8
OUTER_RATE = 0.7
KEEP = 0.9
MESH = pl.DeviceIdType.MESH
BF16 = ml_dtypes.bfloat16


def split_np(a):
    hi = a.astype(np.float32).astype(BF16)
    lo = (a - hi.astype(np.float64)).astype(np.float32).astype(BF16)
    return hi, lo


def cosine_low():
    freq = np.arange(BAND, dtype=np.float64)[:, None]
    place = np.arange(GROUP, dtype=np.float64)[None, :]
    table = np.cos(np.pi * (2.0 * place + 1.0) * freq / (2.0 * GROUP))
    scale = np.where(freq == 0, np.sqrt(1.0 / GROUP), np.sqrt(2.0 / GROUP))
    return table * scale


def tables():
    low = cosine_low()
    diag = np.zeros((4 * GROUP, 4 * BAND))
    for q in range(4):
        diag[q * GROUP : (q + 1) * GROUP, q * BAND : (q + 1) * BAND] = low.T
    hi, lo = split_np(diag)
    col_fwd = np.concatenate([hi, lo], axis=1)
    hi, lo = split_np(diag.T)
    col_inv = np.concatenate([hi, hi, lo], axis=0)
    row_fwd = np.zeros((RING, 2 * BAND, 3 * ROWS_DEV), BF16)
    row_inv = np.zeros((RING, ROWS_DEV, 3 * 2 * BAND), BF16)
    for d in range(RING):
        rows = d * ROWS_DEV + np.arange(ROWS_DEV)
        first, last = rows[0] // GROUP, rows[-1] // GROUP
        part = np.zeros((2 * BAND, ROWS_DEV))
        for slot, b in enumerate((first, last)):
            if slot == 1 and first == last:
                continue
            inside = rows // GROUP == b
            part[slot * BAND : (slot + 1) * BAND, inside] = low[:, rows[inside] % GROUP]
        hi, lo = split_np(part)
        row_fwd[d] = np.concatenate([hi, hi, lo], axis=1)
        hi, lo = split_np(part.T)
        row_inv[d] = np.concatenate([hi, hi, lo], axis=1)
    return col_fwd, col_inv, row_fwd, row_inv


def split(a):
    hi = a.astype(jnp.bfloat16)
    lo = (a - hi.astype(jnp.float32)).astype(jnp.bfloat16)
    return hi, lo


def dot(a, b):
    return jnp.dot(a, b, preferred_element_type=jnp.float32)


def invert(coef, rowi, coli):
    hi, lo = split(coef)
    wide = dot(rowi, jnp.concatenate([hi, lo, hi], axis=0))
    tall = jnp.concatenate([wide[:, 128 * c : 128 * (c + 1)] for c in range(wide.shape[1] // 128)], axis=0)
    hi, lo = split(tall)
    return dot(jnp.concatenate([hi, lo, hi], axis=1), coli)


OWNS = (
    [], [(0, 0, 24)], [(0, 24, 8), (1, 0, 8)], [(1, 8, 8)], [(1, 16, 8)], [(1, 24, 8), (2, 0, 8)], [(2, 8, 16)], [(2, 24, 8)],
)
MEMBERS = ((0, 1, 2), (2, 3, 4, 5), (5, 6, 7))
MOST = 24


def blocks_of(d):
    return [b for b in range(3) if d in MEMBERS[b]]


def share(d, b):
    found = [n for n, own in enumerate(OWNS[d]) if own[0] == b]
    return (found[0], *OWNS[d][found[0]][1:]) if found else (None, 0, 0)


def owned(d):
    return [own[0] for own in OWNS[d]]


def greets(d, b, m):
    return b in owned(d) and not (b == 1 and m in (2, 5))


def greetings(d):
    return sum(greets(m, b, d) for b in blocks_of(d) for m, _ in partners(d, b, (1, 0))) + (4 if OWNS[d] else 0)


def partners(d, b, halves):
    found = [(m, xr) for m in MEMBERS[b] for xr in halves if (m, xr) != (d, 0)]
    return sorted(found, key=lambda p: (-abs(p[0] // 2 - d // 2) - p[1], p[0] == d, p))


def kernel(
    ny, cols,
    inner_in, outer_in, mom_in, res_in, colf_in, coli_in, rowf_in, rowi_in,
    total, res, outer, mom, coli, rowi,
    inner, colf, rowf, part, from_a, sums, from_y, band,
    load_sem, up_sem, ring_sem,
    a_send, a_recv, y_send, y_recv, b_send, b_recv, t_send, t_recv,
):
    hc = cols * BAND // GROUP // 2
    wide = cols // 2
    i, f = lax.axis_index("island"), lax.axis_index("fsdp")
    y, xl = lax.div(i, 2), lax.rem(i, 2)
    d = lax.rem(f, RING)
    base = f - d

    def at(yy, xr, dd):
        return (yy * 2 + (1 - xl if xr else xl), base + dd)

    def ring(k):
        return lax.rem(y + k, ny)

    def signal(sem, where):
        pl.semaphore_signal(sem, 1, device_id=where, device_id_type=MESH)

    def each(devices, body):
        for dd in devices:
            pl.when(d == dd)(functools.partial(body, dd))

    def wide_cols(r):
        return pl.ds(pl.multiple_of((xl if r else 1 - xl) * wide, 128), wide)

    loads = []

    def load(src, dst):
        loads.append(pltpu.make_async_copy(src, dst, load_sem.at[len(loads)]))
        loads[-1].start()

    load(inner_in.at[0, :, wide_cols(0)], inner.at[0])
    load(res_in.at[0, :, wide_cols(0)], res.at[0])
    load(outer_in.at[:, wide_cols(0)], outer.at[0])
    load(colf_in, colf)

    bar = pltpu.get_barrier_semaphore()

    def greet(dd):
        near = [
            (abs(m // 2 - dd // 2) + xr, m, xr) for b in blocks_of(dd) for m, xr in partners(dd, b, (1, 0)) if greets(dd, b, m)
        ]
        for far in (True, False):
            for k in ((2, ny - 2) if far else (1, ny - 1)) if OWNS[dd] else ():
                signal(bar, at(ring(k), 0, dd))
            for hops, m, xr in near:
                if (hops > 1) == far:
                    signal(bar, at(y, xr, m))

    each(range(RING), greet)

    load(inner_in.at[0, :, wide_cols(1)], inner.at[1])
    load(res_in.at[0, :, wide_cols(1)], res.at[1])
    load(outer_in.at[:, wide_cols(1)], outer.at[1])
    load(rowf_in.at[d], rowf)

    @pl.when((d != 2) & (d != 5))
    def _():
        band[:, BAND:] = jnp.zeros((2, BAND, hc), jnp.float32)
        total[BAND:] = jnp.zeros((BAND, 2 * hc), jnp.float32)

    chunks = wide // 512

    def forward():
        pieces = []
        for r in range(2):
            acc = outer[r] - inner[r].astype(jnp.float32) + res[r]
            res[r] = acc
            pieces += [acc[:, 512 * c : 512 * (c + 1)] for c in range(chunks)]
        hi, lo = split(jnp.concatenate(pieces, axis=0))
        prod = dot(hi, colf[...])
        tall = prod[:, :128] + prod[:, 128:] + dot(lo, colf[:, :128])
        hi, lo = split(jnp.concatenate([tall[ROWS_DEV * c : ROWS_DEV * (c + 1)] for c in range(2 * chunks)], axis=1))
        whole = dot(rowf[...], jnp.concatenate([hi, lo, hi], axis=0))
        part[0] = whole[:, :hc]
        part[1] = whole[:, hc:]

    def half_cols():
        return pl.ds(pl.multiple_of(xl * hc, 128), hc)

    def wait_rows(send, recv, rows, count=1):
        ref = part.at[0, :rows] if count == 1 else from_a.at[0, :count, :rows]
        sems = (send, send) if recv is None else (recv, recv)
        copy = pltpu.make_async_remote_copy(ref, ref, *sems, device_id=at(y, 1, d), device_id_type=MESH)
        copy.wait_recv() if recv is not None else copy.wait_send()

    def a_send_half(dd, r, b):
        slot = blocks_of(dd).index(b)
        for to, xr in partners(dd, b, (1 - r,)):
            own, row, rows = share(to, b)
            if not rows:
                continue
            pltpu.make_async_remote_copy(
                part.at[r, slot * BAND + row : slot * BAND + row + rows],
                from_a.at[own, MEMBERS[b].index(dd) * 2 + xr, :rows],
                a_send,
                a_recv.at[own],
                device_id=at(y, xr, to),
                device_id_type=MESH,
            ).start()

    def first_block(dd):
        return 2 if dd == 5 else blocks_of(dd)[0]

    for c in loads[:4]:
        c.wait()
    loads[7].wait()
    for c in loads[4:7]:
        c.wait()
    forward()
    expected = greetings(0)
    for dd in range(1, RING):
        expected = jnp.where(d == dd, greetings(dd), expected)
    pl.semaphore_wait(bar, expected)

    @pl.when((d == 3) | (d == 4))
    def _():
        signal(up_sem, at(y, 0, jnp.where(d == 3, 2, 5)))

    def a_start(dd):
        for r in range(2):
            a_send_half(dd, r, first_block(dd))
        for k in (2, ny - 2) if OWNS[dd] else ():
            signal(ring_sem, at(ring(k), 0, dd))

    each(range(RING), a_start)


    def a_rest(dd):
        pl.semaphore_wait(up_sem, 1)
        for r in range(2):
            a_send_half(dd, r, 1)

    each((2, 5), a_rest)

    load(coli_in, coli)
    load(rowi_in.at[d], rowi)
    load(mom_in, mom)

    def b_copies(dd, b, src, dst, send, recv):
        own, row, rows = share(dd, b)
        for m, xr in partners(dd, b, (1, 0)):
            slot = blocks_of(m).index(b)
            pltpu.make_async_remote_copy(
                src(own, xr, rows),
                dst(xr, slice(slot * BAND + row, slot * BAND + row + rows)),
                send,
                recv.at[slot],
                device_id=at(y, xr, m),
                device_id_type=MESH,
            ).start()

    def own_rows(dd, b):
        start = blocks_of(dd).index(b) * BAND + share(dd, b)[1]
        return slice(start, start + share(dd, b)[2])

    def band_part(xr, at_rows):
        return band.at[1 - xr, at_rows]

    def total_part(xr, at_rows):
        return total.at[at_rows, half_cols()]

    def gather_a(dd):
        for n, (b, row, rows) in enumerate(OWNS[dd]):
            wait_rows(None, a_recv.at[n], rows, 2 * len(MEMBERS[b]) - 1)
            mine, other = part[1, own_rows(dd, b)], None
            for k, m in enumerate(MEMBERS[b]):
                if m != dd:
                    mine = mine + from_a[n, 2 * k, :rows]
                got = from_a[n, 2 * k + 1, :rows]
                other = got if other is None else other + got
            from_y[n, y, :rows] = mine + other
            sums[n, 0, :rows] = mine
            sums[n, 1, :rows] = other
            if n == 0:
                pl.semaphore_wait(ring_sem, 2)
            for k in (4, 3, 5, 2, 6, 1, 7):
                pltpu.make_async_remote_copy(
                    from_y.at[n, y, :rows], from_y.at[n, y, :rows], y_send.at[n], y_recv.at[n],
                    device_id=at(ring(k), 0, dd), device_id_type=MESH,
                ).start()
            b_copies(dd, b, lambda own, xr, rows: sums.at[own, xr, :rows], band_part, b_send, b_recv)
            band[1, own_rows(dd, b)] = mine

    each(range(RING), gather_a)

    def b_wait(recv):
        def go(dd):
            for slot, b in enumerate(blocks_of(dd)):
                wait_rows(None, recv.at[slot], 2 * BAND - share(dd, b)[2])

        each(range(RING), go)

    for c in loads[8:]:
        c.wait()
    b_wait(b_recv)
    sent = invert(jnp.concatenate([band[0], band[1]], axis=1), rowi[...], coli[...])
    for c in range(2 * chunks):
        r, at_c = c // chunks, slice(512 * (c % chunks), 512 * (c % chunks + 1))
        res[r, :, at_c] = res[r, :, at_c] - sent[ROWS_DEV * c : ROWS_DEV * (c + 1)]

    def gather_y(dd):
        for n, (b, row, rows) in enumerate(OWNS[dd]):
            wait_rows(None, y_recv.at[n], rows, ny - 1)
            whole = from_y[n, 0, :rows]
            for k in range(1, ny):
                whole = whole + from_y[n, k, :rows]
            whole = whole * (1.0 / (2 * ny))
            sums[n, 2, :rows] = whole
            b_copies(dd, b, lambda own, xr, rows: sums.at[own, 2, :rows], total_part, t_send, t_recv)
            total[own_rows(dd, b), half_cols()] = whole
        for b in blocks_of(dd):
            wait_rows(a_send, None, 2 * BAND - share(dd, b)[2])
        for n, (b, row, rows) in enumerate(OWNS[dd]):
            wait_rows(y_send.at[n], None, rows, ny - 1)
            for sem in (b_send, t_send):
                wait_rows(sem, None, rows, 2 * len(MEMBERS[b]) - 1)

    each(range(RING), gather_y)
    b_wait(t_recv)


def finish(
    cols,
    total, res, outer, mom, coli, rowi,
    outer_out, mom_out, res_out,
    outer_v, mom_v, out_sem,
):
    xl = lax.rem(lax.axis_index("island"), 2)
    wide = cols // 2
    writes = []

    def write(src, dst):
        writes.append(pltpu.make_async_copy(src, dst, out_sem.at[len(writes)]))
        writes[-1].start()

    def columns(r, n, width):
        return pl.ds(pl.multiple_of(lax.rem(xl + 1 + r, 2) * wide + n, 128), width)

    for r in range(2):
        write(res.at[r], res_out.at[0, :, columns(r, 0, wide)])
    hi, lo = split(total[...])
    half = dot(rowi[...], jnp.concatenate([hi, lo, hi], axis=0))
    step = 1024
    for c in range(cols // step):
        at_c = slice(step * c, step * (c + 1))
        tall = jnp.concatenate([half[:, 128 * q : 128 * (q + 1)] for q in range(c * step // 512, (c + 1) * step // 512)], axis=0)
        hi, lo = split(tall)
        update = dot(jnp.concatenate([hi, lo, hi], axis=1), coli[...])
        for q in range(step // 512):
            n = (c * step + 512 * q) % wide
            r = (c * step + 512 * q) // wide
            at_q = slice(step * c + 512 * q, step * c + 512 * (q + 1))
            u = update[ROWS_DEV * q : ROWS_DEV * (q + 1)]
            rel = jnp.where(r == xl, 1, 0)
            m = KEEP * mom[:, at_q] + u
            mom_v[:, at_q] = m
            outer_v[:, at_q] = outer[rel, :, n : n + 512] - OUTER_RATE * (u + KEEP * m)
        write(mom_v.at[:, at_c], mom_out.at[:, at_c])
        write(outer_v.at[:, at_c], outer_out.at[:, at_c])
    for c in writes:
        c.wait()


def solution(mesh):
    ny = mesh.shape["island"] // 2
    col_fwd, col_inv, row_fwd, row_inv = tables()

    def per_device(inner, outer, momentum, residual):
        rows, cols = outer.shape
        hc = cols * BAND // GROUP // 2
        f32, bf16 = jnp.float32, jnp.bfloat16
        dma, regular = pltpu.SemaphoreType.DMA, pltpu.SemaphoreType.REGULAR
        any_space = pl.BlockSpec(memory_space=pl.ANY)
        vmem = pl.BlockSpec(memory_space=pltpu.VMEM)
        in_hbm = lambda a: pltpu.with_memory_space_constraint(a, pltpu.HBM)
        tables_hbm = [jnp.asarray(a) for a in (col_fwd, col_inv, row_fwd, row_inv)]
        passed = pl.pallas_call(
            functools.partial(kernel, ny, cols),
            name="exchange",
            out_shape=[
                pltpu.VMEM((2 * BAND, 2 * hc), f32),
                pltpu.VMEM((2, rows, cols // 2), f32),
                pltpu.VMEM((2, rows, cols // 2), f32),
                pltpu.VMEM((rows, cols), f32),
                pltpu.VMEM(col_inv.shape, bf16),
                pltpu.VMEM(row_inv.shape[1:], bf16),
            ],
            in_specs=[any_space] * 8,
            out_specs=[vmem] * 6,
            scratch_shapes=[
                pltpu.VMEM((2, rows, cols // 2), bf16),
                pltpu.VMEM(col_fwd.shape, bf16),
                pltpu.VMEM(row_fwd.shape[1:], bf16),
                pltpu.VMEM((2, 2 * BAND, hc), f32),
                pltpu.VMEM((2, 8, MOST, hc), f32),
                pltpu.VMEM((2, 3, MOST, hc), f32),
                pltpu.VMEM((2, ny, MOST, hc), f32),
                pltpu.VMEM((2, 2 * BAND, hc), f32),
                dma((11,)), regular, regular,
                dma, dma((2,)), dma((2,)), dma((2,)), dma, dma((2,)), dma, dma((2,)),
            ],
            compiler_params=pltpu.CompilerParams(
                collective_id=0, has_side_effects=True, vmem_limit_bytes=24 * 1024 * 1024
            ),
        )(*map(in_hbm, (inner, outer, momentum, residual, *tables_hbm)))
        return tuple(
            pl.pallas_call(
                functools.partial(finish, cols),
                name="finish",
                out_shape=[
                    jax.ShapeDtypeStruct((rows, cols), f32),
                    jax.ShapeDtypeStruct((rows, cols), f32),
                    jax.ShapeDtypeStruct((1, rows, cols), f32),
                ],
                in_specs=[vmem] * 6,
                out_specs=[any_space] * 3,
                scratch_shapes=[pltpu.VMEM((rows, cols), f32), pltpu.VMEM((rows, cols), f32), dma((8,))],
                compiler_params=pltpu.CompilerParams(vmem_limit_bytes=24 * 1024 * 1024),
            )(*passed)
        )

    return jax.shard_map(
        per_device,
        mesh=mesh,
        in_specs=(P("island", "fsdp", None), P("fsdp", None), P("fsdp", None), P("island", "fsdp", None)),
        out_specs=(P("fsdp", None), P("fsdp", None), P("island", "fsdp", None)),
        check_vma=False,
    )
```
